256 devices in a mesh: emb: 128 (over y, x, z), nn: 2 (over core).
Axes of the slice: x: 4, y: 4, z: 8, core: 2. Of those that a mesh axis runs over, the one named last changes fastest.
Arguments:
- dense_input: bfloat16 [2, 32768, 128], P(None, ('emb', 'nn')), may hold values from -6 to 6
- id_owner: int32 [2, 393216, 1], P(None, ('emb', 'nn')), may hold values from 0 to 127; in each aligned block of 1536 rows (0 to 1535, 1536 to 3071, ..., all dimensions but the last counted through in order) at most 24 rows name the same one
- id_row: int32 [2, 256, 1536], P(None, ('emb', 'nn')), may hold values from 0 to 1023
- id_mask: int32 [2, 256, 1536], P(None, ('emb', 'nn')), may hold values 0 or 1
- bag_index: int32 [2, 256, 1536], P(None, ('emb', 'nn')), may hold values from 0 to 511, never falling along the last dimension, each value on 1 to 8 neighbouring positions
- labels: int32 [2, 32768], P(None, ('emb', 'nn')), may hold values from 0 to 1
- stale_owner: int32 [2, 393216, 1], P(None, ('emb', 'nn')), may hold values from 0 to 127; in each aligned block of 1536 rows (0 to 1535, 1536 to 3071, ..., all dimensions but the last counted through in order) at most 24 rows name the same one
- stale_row: int32 [2, 256, 1536], P(None, ('emb', 'nn')), may hold values from 0 to 1023
- stale_grad: bfloat16 [2, 256, 1536, 128], P(None, ('emb', 'nn')), may hold values from -6 to 6
- emb_table: float32 [131072, 128], P('emb'), may hold values from -3 to 3
- grad_squares: float32 [131072, 128], P('emb'), may hold values from 0.1 to 1
- bottom_first: bfloat16 [128, 512], replicated, may hold values from -0.5 to 0.5
- bottom_bias: float32 [512], replicated, may hold values from -3 to 3
- bottom_second: bfloat16 [512, 128], replicated, may hold values from -0.25 to 0.25
- top_weight: bfloat16 [640, 4096], replicated, may hold values from -0.25 to 0.25
- top_bias: float32 [4096], replicated, may hold values from -3 to 3
- out_weight: bfloat16 [4096], replicated, may hold values from -0.09375 to 0.09375
- top_squares: float32 [640, 4096], P('nn', 'emb'), may hold values from 1000 to 30000
Outputs:
- row_grads: bfloat16 [2, 256, 1536, 128], P(None, ('emb', 'nn'))
- new_table: float32 [131072, 128], P('emb')
- new_squares: float32 [131072, 128], P('emb')
- top_step: float32 [640, 4096], P('nn', 'emb')
The draws below stay inside these ranges and needn't reach their ends.
Inputs may be any that keep to these rules, and one draw needn't show every extreme that they name: `id_owner`: in each aligned block of 1536 rows (one list of one micro-batch) no owner is named more than 24 times, a bound that some block reaches. `bag_index`: along each list, bag numbers never fall and each of the 512 bags holds 1 to 8 slots, some bag exactly 8. `stale_owner`: in each aligned block of 1536 rows no owner is named more than 24 times, a bound that some block reaches.
All inputs are finite; a program needn't handle non-finite values. No bound on the sum of `id_mask` on one device may be relied on, other than what follows from the above.
Results may differ from the reference program's by a relative error of at most 0.0055.
Values may be sent and summed in bfloat16 or wider, within the bound.
No kernel may reach another device: no remote copies, remote signals or barrier semaphores. Data moves between devices by JAX's collectives and lax.ppermute only.
A program may use at most 128 MiB of HBM per device.

```python
import math
import jax
import jax.numpy as jnp
import numpy as np
from jax import lax

EMB = 128
FEATS = 4
DENSE = 128
BOTTOM = 512
TOP = 4096
JOINED = 640
MB = 2
SAMP = 128
BAGS = 512
LIST = 1536
CAP = 24
BAG_MOST = 8
ROWS_DEV = 1024
TABLE_ROWS = 131072
N_EMB = 128
N_NN = 2


def with_ends(values, stream_key, smallest, high):
    index_at = [jax.random.randint(jax.random.fold_in(stream_key, axis), (), 0, length) for axis, length in enumerate(values.shape)]
    main_axis = values.shape.index(max(values.shape))
    beside = index_at[:main_axis] + [(index_at[main_axis] + 1) % values.shape[main_axis]] + index_at[main_axis + 1:]
    return values.at[tuple(index_at)].set(smallest).at[tuple(beside)].set(high)


def steps_of(stream_key, extent, shards, low, high):
    loudness = 1.0
    for axis_at, parts in shards:
        steps = jax.random.uniform(jax.random.fold_in(jax.random.fold_in(stream_key, 6), axis_at), (parts,), jnp.float32, low / len(shards), high / len(shards))
        loudness = loudness * jnp.repeat(jnp.exp(steps), extent[axis_at] // parts).reshape((-1,) + (1,) * (len(extent) - 1 - axis_at))
    return loudness


def split_up(number_of, total, reach, slope):
    loads = [(1 << 20) // math.isqrt(grade ** slope) + 1 for grade in range(2, number_of + 1)]
    surplus, holding = total - reach - (number_of - 1), [1] * (number_of - 1)
    while surplus > 0:
        candidates = [i for i in range(number_of - 1) if holding[i] < reach]
        whole, budget = sum([loads[i] for i in candidates]), surplus
        for i in candidates:
            extra = min(reach - holding[i], max(1, budget * loads[i] // whole), surplus)
            holding[i] = holding[i] + extra
            surplus = surplus - extra
    return np.array([reach] + holding)


def ragged(key, count, total, reach, skew):
    if count == 2:
        one = jax.random.randint(key, (), max(1, total - reach), min(reach, total - 1) + 1)
        return jnp.stack([one, total - one])
    lengths = jnp.asarray(split_up(count, total, reach, skew), jnp.int32)
    pairs = (count - 1) // 2
    donor, sink = lengths[1:1 + 2 * pairs:2], lengths[2:2 + 2 * pairs:2]
    slack = jnp.minimum(donor - 1, reach - sink)
    shifted = jax.random.randint(jax.random.fold_in(key, 1), (pairs,), 0, 1 << 20) % (slack + 1)
    lengths = lengths.at[1:1 + 2 * pairs:2].set(donor - shifted).at[2:2 + 2 * pairs:2].set(sink + shifted)
    return lengths[jax.random.permutation(jax.random.fold_in(key, 2), count)]


def deal_out(key, own, number, rows, amount, top, reach, lean):
    order = jax.random.permutation(key, amount)
    crowded, usual = load_shares(amount, rows * top, reach, lean, True), load_shares(amount, rows * top, reach, lean, False)
    places = jnp.arange(amount)

    def named(sizes, rotation):
        used = int((sizes > 0).sum())
        fixed = max(1, used // 4)
        shifted = fixed + (places - fixed + rotation * (used - fixed)) % max(1, amount - fixed)
        return jnp.zeros((amount,), jnp.int32).at[order[jnp.where(places < fixed, places, shifted)]].set(jnp.asarray(sizes, jnp.int32))

    sizes = jnp.where(number % 4 == 0, named(crowded, number // 4), named(usual, number - number // 4 - 1))
    mixed = jax.random.permutation(jax.random.fold_in(own, 3), amount)
    source_of, taker = mixed[0:amount // 2 * 2:2], mixed[1:amount // 2 * 2:2]
    room = jnp.minimum(sizes[source_of] - 1, reach - sizes[taker]) // 2
    room = jnp.where((source_of == order[0]) | (taker == order[0]) | (sizes[taker] == 0), 0, jnp.maximum(room, 0))
    shifted = jax.random.randint(jax.random.fold_in(own, 4), (amount // 2,), 0, 1 << 20) % (room + 1)
    sizes = sizes.at[source_of].add(-shifted).at[taker].add(shifted)
    items = jnp.searchsorted(jnp.cumsum(sizes), jnp.arange(rows * top), side="right").astype(jnp.int32)
    listing = items.reshape(top, rows).T
    listing = listing[jax.random.permutation(jax.random.fold_in(own, 1), rows)]
    rotation = jax.random.randint(jax.random.fold_in(own, 2), (rows, 1), 0, top)
    return jnp.take_along_axis(listing, (jnp.arange(top)[None, :] + rotation) % top, axis=1)


def load_shares(amount, total, reach, skew, full):
    weights = [(1 << 20) // math.isqrt(grade ** skew) + 1 for grade in range(1, amount + 1)]
    largest = reach if full else min(reach, max(-(-total // amount), total * weights[0] // sum(weights)))
    least = 1 if total - largest >= amount - 1 else 0
    holding, surplus = [largest] + [least] * (amount - 1), total - largest - least * (amount - 1)
    while surplus > 0:
        free = [i for i in range(1, amount) if holding[i] < largest] or [i for i in range(1, amount) if holding[i] < reach]
        whole, left = sum([weights[i] for i in free]), surplus
        for i in free:
            addition = min(reach - holding[i], max(1, left * weights[i] // whole), surplus)
            holding[i] = holding[i] + addition
            surplus = surplus - addition
    return np.array(holding)


def gaussian(key, extent, scale, most, cuts=(), dtype=jnp.bfloat16):
    drawn = jax.random.normal(key, extent, jnp.float32) * scale
    if len(cuts) > 0:
        drawn = steps_of(key, extent, cuts, -0.22, 0.18) * drawn
    return jnp.clip(drawn, min=-most, max=most).astype(dtype)


def setup_inputs(seed: int = 0) -> dict:
    seeds = jax.random.split(jax.random.key(seed), 19)
    dense_input = gaussian(seeds[0], (MB, N_EMB * N_NN * SAMP, DENSE), 1.0, 6.0, ((1, 256),))
    id_owner_keys = jax.random.split(jax.random.fold_in(seeds[1], 1), MB * (N_EMB * N_NN * LIST) // LIST)
    id_owner_turns = jax.random.permutation(jax.random.fold_in(seeds[1], 3), MB * (N_EMB * N_NN * LIST) // LIST)
    id_owner = jax.vmap(lambda own, number: deal_out(jax.random.fold_in(seeds[1], 2), own, number, LIST, N_EMB, 1, CAP, 2))(id_owner_keys, id_owner_turns).reshape((MB, N_EMB * N_NN * LIST, 1))
    id_row = with_ends(jax.random.randint(seeds[2], (MB, N_EMB * N_NN, LIST), 0, ROWS_DEV), jax.random.fold_in(seeds[2], 1), 0, ROWS_DEV - 1).astype(jnp.int32)
    id_mask = with_ends((jax.random.randint(seeds[3], (MB, N_EMB * N_NN, LIST), 0, 8) < 7).astype(jnp.int32), jax.random.fold_in(seeds[3], 1), 0, 1)
    bag_index = jax.vmap(lambda own: jnp.searchsorted(jnp.cumsum(ragged(own, BAGS, LIST, BAG_MOST, 1)), jnp.arange(LIST), side="right"))(jax.random.split(seeds[4], MB * (N_EMB * N_NN))).reshape((MB, N_EMB * N_NN, LIST)).astype(jnp.int32)
    labels = with_ends(jax.random.randint(seeds[5], (MB, N_EMB * N_NN * SAMP), 0, 2), jax.random.fold_in(seeds[5], 1), 0, 1).astype(jnp.int32)
    stale_owner_keys = jax.random.split(jax.random.fold_in(seeds[6], 1), MB * (N_EMB * N_NN * LIST) // LIST)
    stale_owner_turns = jax.random.permutation(jax.random.fold_in(seeds[6], 3), MB * (N_EMB * N_NN * LIST) // LIST)
    stale_owner = jax.vmap(lambda own, number: deal_out(jax.random.fold_in(seeds[6], 2), own, number, LIST, N_EMB, 1, CAP, 2))(stale_owner_keys, stale_owner_turns).reshape((MB, N_EMB * N_NN * LIST, 1))
    stale_row = with_ends(jax.random.randint(seeds[7], (MB, N_EMB * N_NN, LIST), 0, ROWS_DEV), jax.random.fold_in(seeds[7], 1), 0, ROWS_DEV - 1).astype(jnp.int32)
    stale_grad = gaussian(seeds[8], (MB, N_EMB * N_NN, LIST, EMB), 1.0, 6.0, ((1, 256),))
    emb_table = gaussian(seeds[9], (TABLE_ROWS, EMB), 0.5, 3.0, ((0, 128),), jnp.float32)
    grad_squares = jnp.clip(jnp.exp(math.log(1.0) - 2.3025851 * jax.random.uniform(seeds[10], (TABLE_ROWS, EMB), jnp.float32) ** steps_of(seeds[10], (TABLE_ROWS, EMB), ((0, 128),), -0.2, 0.2)), 0.1, 1.0)
    bottom_first = gaussian(seeds[11], (DENSE, BOTTOM), DENSE ** -0.5, 0.5)
    bottom_bias = gaussian(seeds[12], (BOTTOM,), 0.5, 3.0, (), jnp.float32)
    bottom_second = gaussian(seeds[13], (BOTTOM, EMB), BOTTOM ** -0.5, 0.25)
    top_weight = gaussian(seeds[14], (JOINED, TOP), JOINED ** -0.5, 0.25)
    top_bias = gaussian(seeds[15], (TOP,), 0.5, 3.0, (), jnp.float32)
    out_weight = gaussian(seeds[16], (TOP,), TOP ** -0.5, 0.09375)
    top_squares = jnp.clip(jnp.exp(math.log(30000.0) - 3.4011974 * jax.random.uniform(seeds[17], (JOINED, TOP), jnp.float32) ** steps_of(seeds[17], (JOINED, TOP), ((0, 2), (1, 128)), -0.2, 0.2)), 1000.0, 30000.0)
    return dict(dense_input=dense_input, id_owner=id_owner, id_row=id_row, id_mask=id_mask, bag_index=bag_index, labels=labels, stale_owner=stale_owner, stale_row=stale_row, stale_grad=stale_grad, emb_table=emb_table, grad_squares=grad_squares, bottom_first=bottom_first, bottom_bias=bottom_bias, bottom_second=bottom_second, top_weight=top_weight, top_bias=top_bias, out_weight=out_weight, top_squares=top_squares)


LEARN_RATE = 0.1
LOSS_SCALE = 64.0

def dense_pass(dense_rows, label_rows, pooled, bottom_first, bottom_bias, bottom_second, top_weight, top_bias, out_weight):
    hidden = jax.nn.relu(jnp.dot(dense_rows, bottom_first, preferred_element_type=jnp.float32) + bottom_bias).astype(jnp.bfloat16)
    bottom = jax.nn.relu(jnp.dot(hidden, bottom_second, preferred_element_type=jnp.float32))
    joined = jnp.concatenate([bottom, pooled], axis=1).astype(jnp.bfloat16)
    before = jnp.dot(joined, top_weight, preferred_element_type=jnp.float32) + top_bias
    gate_value = jax.nn.sigmoid(before)
    active = (before * gate_value).astype(jnp.bfloat16)
    logits = jnp.dot(active, out_weight, preferred_element_type=jnp.float32)
    logit_grad = LOSS_SCALE * (jax.nn.sigmoid(logits) - label_rows.astype(jnp.float32))
    top_delta = (logit_grad[:, None] * out_weight.astype(jnp.float32)[None, :] * gate_value * (1.0 + before * (1.0 - gate_value))).astype(jnp.bfloat16)
    split_at = bottom.shape[1]
    back_grad = lax.dot_general(top_delta, top_weight[split_at:], (((1,), (1,)), ((), ())), preferred_element_type=jnp.float32)
    return (joined, top_delta, back_grad)

def pool_one(fetched_rows, bag_rows):
    return jax.ops.segment_sum(fetched_rows, bag_rows, num_segments=BAGS, indices_are_sorted=True)

def pick_one(bag_rows, bag_ids):
    return jnp.take(bag_rows, bag_ids, axis=0)

def reference(dense_input, id_owner, id_row, id_mask, bag_index, labels, stale_owner, stale_row, stale_grad, emb_table, grad_squares, bottom_first, bottom_bias, bottom_second, top_weight, top_bias, out_weight, top_squares):
    devices = N_EMB * N_NN
    table_half = emb_table.astype(jnp.bfloat16)
    dense_all = jnp.swapaxes(dense_input.reshape(MB, devices, SAMP, DENSE), 0, 1)
    label_all = jnp.swapaxes(labels.reshape(MB, devices, SAMP), 0, 1)
    owner_all = jnp.swapaxes(id_owner.reshape(MB, devices, LIST), 0, 1)
    row_all = jnp.swapaxes(id_row, 0, 1)
    mask_all = jnp.swapaxes(id_mask, 0, 1)
    bag_all = jnp.swapaxes(bag_index, 0, 1)
    old_owner_all = jnp.swapaxes(stale_owner.reshape(MB, devices, LIST), 0, 1)
    old_row_all = jnp.swapaxes(stale_row, 0, 1)
    old_grad_all = jnp.swapaxes(stale_grad, 0, 1)

    def device_step(carry, pieces):
        grad_total, row_sum = carry
        dense_part, label_part, owner_part, row_part, mask_part, bag_part, old_owner, old_row, old_grad = pieces
        index = owner_part * ROWS_DEV + row_part
        live_mask = mask_part.astype(jnp.float32)[..., None]
        fetched = jnp.take(table_half, index, axis=0).astype(jnp.float32) * live_mask
        pooled = jax.vmap(pool_one)(fetched, bag_part).reshape(MB * SAMP, FEATS * EMB)
        joined, top_delta, back_grad = dense_pass(dense_part.reshape(MB * SAMP, DENSE), label_part.reshape(MB * SAMP), pooled, bottom_first, bottom_bias, bottom_second, top_weight, top_bias, out_weight)
        term = lax.dot_general(joined, top_delta, (((0,), (0,)), ((), ())), preferred_element_type=jnp.float32)
        bag_grad = back_grad.reshape(MB, BAGS, EMB)
        grads_here = (jax.vmap(pick_one)(bag_grad, bag_part) * live_mask).astype(jnp.bfloat16)
        old_index = (old_owner * ROWS_DEV + old_row).reshape(MB * LIST)
        row_sum = row_sum.at[old_index].add(old_grad.reshape(MB * LIST, EMB).astype(jnp.float32))
        return ((grad_total + term, row_sum), grads_here)
    start_carry = (jnp.zeros((JOINED, TOP), jnp.float32), jnp.zeros((TABLE_ROWS, EMB), jnp.float32))
    (top_grad, row_sum), grads_all = lax.scan(device_step, start_carry, (dense_all, label_all, owner_all, row_all, mask_all, bag_all, old_owner_all, old_row_all, old_grad_all))
    row_grads = jnp.swapaxes(grads_all, 0, 1)
    top_step = top_grad * lax.rsqrt(top_squares + top_grad * top_grad)
    new_squares = grad_squares + row_sum * row_sum
    new_table = emb_table - LEARN_RATE * row_sum * lax.rsqrt(new_squares)
    return (row_grads, new_table, new_squares, top_step)
```

```python
import functools

import jax
import jax.numpy as jnp
from jax import lax
from jax.experimental import pallas as pl
from jax.experimental.pallas import tpu as pltpu
from jax.sharding import Mesh, PartitionSpec as P

FEATS = 4
CAP = 24
RING = 8
LEARN_RATE = 0.1
LOSS_SCALE = 64.0
LANES = 128
VMEM = 48 * 1024 * 1024
BF = jnp.bfloat16
F32 = jnp.float32
I32 = jnp.int32


def iota(shape, axis):
    return lax.broadcasted_iota(I32, shape, axis)


def ones_where(cond):
    return jnp.where(cond, 1.0, 0.0).astype(BF)


def mm(a, b):
    return jnp.dot(a, b, preferred_element_type=F32)


def call(body, out_shape, scratch=(), **more):
    return pl.pallas_call(
        body,
        out_shape=out_shape,
        scratch_shapes=scratch,
        compiler_params=pltpu.CompilerParams(vmem_limit_bytes=VMEM),
        **more,
    )


def nt(a, b):
    return lax.dot_general(a, b, (((1,), (1,)), ((), ())), preferred_element_type=F32)


def route_body(owner_ref, old_owner_ref, row_ref, old_row_ref, bag_ref, req_ref, bagpos_ref, pos_ref):
    peers = req_ref.shape[0]
    length = owner_ref.shape[2]
    chunk = 256 if length % 256 == 0 else length
    upper = ones_where(iota((chunk, chunk), 0) <= iota((chunk, chunk), 1))
    zero = jnp.zeros((LANES, length), F32)
    total = jnp.zeros((peers, LANES), F32)
    bag_total = jnp.zeros((peers, LANES), F32)
    for turn in range(4):
        mb = turn % 2
        own = (owner_ref if turn < 2 else old_owner_ref)[mb]
        row = (row_ref if turn < 2 else old_row_ref)[mb] + 1
        hit = own == iota((peers, length), 0)
        onehot = ones_where(hit)
        carry = jnp.zeros((peers, 1), F32)
        parts = []
        for at in range(0, length, chunk):
            counted = mm(onehot[:, at : at + chunk], upper) + carry
            carry = counted[:, chunk - 1 :]
            parts.append(counted)
        counted = jnp.concatenate(parts, axis=1)
        rank = jnp.sum(jnp.where(hit, counted, 0.0), axis=0, keepdims=True).astype(I32) - 1
        place = iota((LANES, length), 0) == rank + turn * CAP

        def spread(value):
            high = jnp.where(place, (value >> 5).astype(F32), zero).astype(BF)
            low = jnp.where(place, (value & 31).astype(F32), zero).astype(BF)
            return nt(onehot, high) * 32.0 + nt(onehot, low)

        total += spread(row)
        if turn < 2:
            bag_total += spread(bag_ref[mb])
        else:
            pos_ref[mb] = own * CAP + rank
    req_ref[...] = total.astype(I32) - 1
    bagpos_ref[...] = bag_total.astype(I32) - 1


def gather_body(z_ref, req_ref, mine_ref, other_ref, first_ref, second_ref, cols_ref, hot_ref, out_ref):
    groups = first_ref.shape[0]
    ring = mine_ref.shape[0]
    half = mine_ref.shape[1]
    both = 2 * CAP
    for z in range(ring):
        part = req_ref[pl.ds(z, groups, stride=ring), :]
        part = jnp.concatenate([part, jnp.zeros((LANES - groups, LANES), I32)], axis=0)
        cols_ref[z] = part.T
    me = z_ref[0]

    def step(pair, carry):
        for zi in range(2):
            z = pair * 2 + zi
            offset = lax.rem(me - z + ring, ring)
            cols = cols_ref[z]
            for w in range(groups):
                hot_ref[w * both : (w + 1) * both, :] = ones_where(
                    cols[:both, w : w + 1] == iota((both, 2 * half), 1)
                )
            found = mm(hot_ref[:, :half], mine_ref[offset]) + mm(hot_ref[:, half:], other_ref[offset])
            out_ref[zi] = found.reshape(groups, both, LANES)
        for mb, ref in enumerate((first_ref, second_ref)):
            ref[:, pl.ds(pl.multiple_of(pair * both, both), both), :] = jnp.concatenate(
                [out_ref[zi, :, mb * CAP : (mb + 1) * CAP, :] for zi in range(2)], axis=1
            ).astype(BF)
        return carry

    lax.fori_loop(0, ring // 2, step, 0)


def pool_body(bagpos_ref, reply_ref, out_ref):
    groups, per, width = reply_ref.shape
    samples = out_ref.shape[0]
    bags = samples * FEATS
    flat = reply_ref[...].reshape(groups * per, width)
    size = 2 * per
    total = jnp.zeros((bags, width), F32)
    for at in range(0, groups * per, size):
        hot = ones_where(bagpos_ref[:, at : at + size] == iota((bags, size), 0))
        total += mm(hot, flat[at : at + size])
    for feat in range(FEATS):
        out_ref[:, feat * width : (feat + 1) * width] = total[
            feat * samples : (feat + 1) * samples
        ].astype(BF)


def outgoing_body(pos_ref, grad_ref, out_ref):
    here, _, per, width = out_ref.shape
    length = pos_ref.shape[2]
    first = pl.program_id(0) * here * per
    for mb in range(2):
        pos = pos_ref[mb] - first
        for w in range(here):
            hot = ones_where(pos == iota((per, length), 0) + w * per)
            out_ref[w, mb] = mm(hot, grad_ref[mb]).astype(BF)


def scatter_body(rows_ref, grad_ref, out_ref):
    groups = grad_ref.shape[0]
    width = grad_ref.shape[3]
    table_rows = out_ref.shape[1]
    wide = grad_ref[...].astype(F32)
    count = groups * 2 * CAP
    for zi in range(2):
        part = wide[:, :, zi * CAP : (zi + 1) * CAP, :].reshape(count, width).astype(BF)
        hot = ones_where(rows_ref[zi] == iota((table_rows, count), 0))
        out_ref[zi] = mm(hot, part)


def pick_body(bag_ref, back_ref, out_ref):
    samples = back_ref.shape[0] // 2
    bags = samples * FEATS
    length = bag_ref.shape[2]
    width = back_ref.shape[1] // FEATS
    for mb in range(2):
        rows = back_ref[mb * samples : (mb + 1) * samples, :]
        grads = jnp.concatenate(
            [rows[:, feat * width : (feat + 1) * width] for feat in range(FEATS)], axis=0
        ).astype(BF)
        for at in range(0, length, LANES):
            ids = jnp.broadcast_to(bag_ref[mb, :, at : at + LANES], (LANES, LANES)).T
            hot = jnp.concatenate(
                [ones_where(ids == iota((LANES, LANES), 1) + block) for block in range(0, bags, LANES)],
                axis=1,
            )
            out_ref[mb, 0, at : at + LANES, :] = mm(hot, grads).astype(BF)


def shape_of(shape, dtype):
    return jax.ShapeDtypeStruct(shape, dtype)


def ring_of(size, shift):
    return [(i, (i + shift) % size) for i in range(size)]


def per_device(
    dense_input,
    id_owner,
    id_row,
    id_mask,
    bag_index,
    labels,
    stale_owner,
    stale_row,
    stale_grad,
    emb_table,
    grad_squares,
    bottom_first,
    bottom_bias,
    bottom_second,
    top_weight,
    top_bias,
    out_weight,
    top_squares,
):
    groups = lax.axis_size("w")
    ring = lax.axis_size("z")
    peers = groups * ring
    core = lax.axis_index("nn")
    my_z = lax.axis_index("z")
    swap = [(0, 1), (1, 0)]
    length = id_row.shape[2]
    width = emb_table.shape[1]
    table_rows = emb_table.shape[0]
    half_rows = table_rows // 2
    samples = dense_input.shape[1]
    bags = samples * FEATS
    per = ring * CAP

    my_half = lax.dynamic_slice_in_dim(emb_table, core * half_rows, half_rows, 0).astype(BF)
    blocks = [my_half]
    ahead, back = my_half, my_half
    behind = []
    for step in range(1, ring // 2 + 1):
        ahead = lax.ppermute(ahead, "z", ring_of(ring, 1))
        blocks.append(ahead)
        if step < ring - ring // 2:
            back = lax.ppermute(back, "z", ring_of(ring, -1))
            behind.append(back)
    mine_table = jnp.stack(blocks + behind[::-1])
    other_table = lax.ppermute(mine_table, "nn", swap)

    bag_order = (bag_index & (FEATS - 1)) * samples + (bag_index >> 2)
    bag_or_none = jnp.where(id_mask > 0, bag_order + 1, 0)
    requests, bagpos, old_pos = call(
        route_body,
        (
            shape_of((peers, LANES), I32),
            shape_of((peers, LANES), I32),
            shape_of((2, 1, length), I32),
        ),
    )(
        id_owner.reshape(2, 1, length),
        stale_owner.reshape(2, 1, length),
        id_row,
        stale_row,
        bag_or_none,
    )
    asked = lax.all_to_all(requests, "w", split_axis=0, concat_axis=0, tiled=True)
    bag_rows = (
        bagpos[:, : 2 * CAP].reshape(peers, 2, CAP).transpose(1, 0, 2).reshape(2, 1, peers * CAP)
    )
    old_rows = (
        asked[:, 2 * CAP : 4 * CAP]
        .reshape(groups, ring, 2 * CAP)
        .transpose(1, 0, 2)
        .reshape(ring, 1, groups * 2 * CAP)
    )
    wanted = jnp.where(asked >= 0, asked ^ (core * half_rows), -1)

    replies = call(
        gather_body,
        tuple(shape_of((groups, per, width), BF) for _ in range(2)),
        (
            pltpu.VMEM((ring, LANES, LANES), I32),
            pltpu.VMEM((groups * 2 * CAP, table_rows), BF),
            pltpu.VMEM((2, groups, 2 * CAP, width), F32),
        ),
        in_specs=[pl.BlockSpec(memory_space=pltpu.SMEM)] + [pl.BlockSpec()] * 3,
    )(my_z.reshape(1), wanted, mine_table, other_table)
    pooled = []
    for mb in range(2):
        here = lax.all_to_all(replies[mb], "w", split_axis=0, concat_axis=0, tiled=True)
        pooled.append(call(pool_body, shape_of((samples, FEATS * width), BF))(bag_rows[mb], here))
    pooled = jnp.concatenate(pooled, axis=0)

    cut = 4
    outgoing = call(
        outgoing_body,
        shape_of((groups, 2, per, width), BF),
        grid=(cut,),
        in_specs=[
            pl.BlockSpec((2, 1, length), lambda i: (0, 0, 0)),
            pl.BlockSpec((2, length, width), lambda i: (0, 0, 0)),
        ],
        out_specs=pl.BlockSpec((groups // cut, 2, per, width), lambda i: (i, 0, 0, 0)),
    )(old_pos, stale_grad.reshape(2, length, width))
    incoming = lax.all_to_all(outgoing, "w", split_axis=0, concat_axis=0, tiled=True)
    sums = call(
        scatter_body,
        shape_of((ring, table_rows, width), F32),
        grid=(ring // 2,),
        in_specs=[
            pl.BlockSpec((2, 1, groups * 2 * CAP), lambda i: (i, 0, 0)),
            pl.BlockSpec((groups, 2, 2 * CAP, width), lambda i: (0, 0, i, 0)),
        ],
        out_specs=pl.BlockSpec((2, table_rows, width), lambda i: (i, 0, 0)),
    )(old_rows, incoming)
    sums = sums.reshape(ring, 2, half_rows, width)
    theirs = lax.dynamic_index_in_dim(sums, 1 - core, 1, keepdims=False)
    ours = lax.dynamic_index_in_dim(sums, core, 1, keepdims=False)
    ours = (ours + lax.ppermute(theirs, "nn", swap)).astype(BF)
    ours = lax.all_to_all(ours, "z", split_axis=0, concat_axis=0, tiled=True)
    ours = jnp.sum(ours.astype(F32), axis=0)
    theirs = lax.ppermute(ours, "nn", swap)
    row_sum = jnp.where(
        core == 0,
        jnp.concatenate([ours, theirs], axis=0),
        jnp.concatenate([theirs, ours], axis=0),
    )
    new_squares = grad_squares + row_sum * row_sum
    new_table = emb_table - LEARN_RATE * row_sum * lax.rsqrt(new_squares)

    dense_rows = dense_input.reshape(2 * samples, dense_input.shape[2])
    label_rows = labels.reshape(2 * samples)
    hidden = jax.nn.relu(mm(dense_rows, bottom_first) + bottom_bias).astype(BF)
    bottom = jax.nn.relu(mm(hidden, bottom_second)).astype(BF)
    joined = jnp.concatenate([bottom, pooled], axis=1)
    before = mm(joined, top_weight) + top_bias
    gate = jax.nn.sigmoid(before)
    active = (before * gate).astype(BF)
    logits = mm(active, out_weight)
    logit_grad = LOSS_SCALE * (jax.nn.sigmoid(logits) - label_rows.astype(F32))
    top_delta = (
        logit_grad[:, None]
        * out_weight.astype(F32)[None, :]
        * gate
        * (1.0 + before * (1.0 - gate))
    ).astype(BF)
    split_at = bottom.shape[1]
    back_grad = nt(top_delta, top_weight[split_at:])
    row_grads = call(pick_body, shape_of((2, 1, length, width), BF))(bag_or_none - 1, back_grad)

    inputs = joined.shape[1] // 2

    def outer(at):
        part = lax.dynamic_slice_in_dim(joined, at * inputs, inputs, 1)
        return lax.dot_general(top_delta, part, (((0,), (0,)), ((), ())), preferred_element_type=F32)

    sent = lax.ppermute(outer(1 - core).astype(BF), "nn", swap)
    unit_part = (outer(core) + sent.astype(F32)).astype(BF)
    units = unit_part.shape[0] // peers
    unit_part = lax.all_to_all(
        unit_part.reshape(groups, ring * units, inputs), "w", split_axis=0, concat_axis=0, tiled=True
    )
    unit_part = jnp.sum(unit_part.astype(F32), axis=0).astype(BF).reshape(ring, units, inputs)
    unit_part = lax.all_to_all(unit_part, "z", split_axis=0, concat_axis=0, tiled=True)
    top_grad = jnp.sum(unit_part.astype(F32), axis=0).T
    top_step = top_grad * lax.rsqrt(top_squares + top_grad * top_grad)
    return (row_grads, new_table, new_squares, top_step)


def solution(mesh, ring=RING):
    devices = mesh.devices
    fine = Mesh(devices.reshape(devices.shape[0] // ring, ring, devices.shape[1]), ("w", "z", "nn"))
    rows = ("w", "z", "nn")
    emb = ("w", "z")
    return jax.shard_map(
        per_device,
        mesh=fine,
        in_specs=(
            P(None, rows, None),
            P(None, rows, None),
            P(None, rows, None),
            P(None, rows, None),
            P(None, rows, None),
            P(None, rows),
            P(None, rows, None),
            P(None, rows, None),
            P(None, rows, None, None),
            P(emb, None),
            P(emb, None),
            P(),
            P(),
            P(),
            P(),
            P(),
            P(),
            P("nn", emb),
        ),
        out_specs=(
            P(None, rows, None, None),
            P(emb, None),
            P(emb, None),
            P("nn", emb),
        ),
        check_vma=False,
    )
```

```python
import functools

import jax
import jax.numpy as jnp
from jax import lax
from jax.experimental import pallas as pl
from jax.experimental.pallas import tpu as pltpu
from jax.sharding import Mesh, PartitionSpec as P

FEATS = 4
CAP = 24
RING = 8
LEARN_RATE = 0.1
LOSS_SCALE = 64.0
LANES = 128
VMEM = 24 * 1024 * 1024
BF = jnp.bfloat16
F32 = jnp.float32
I32 = jnp.int32


def iota(shape, axis):
    return lax.broadcasted_iota(I32, shape, axis)


def ones_where(cond):
    return jnp.where(cond, 1.0, 0.0).astype(BF)


def mm(a, b):
    return jnp.dot(a, b, preferred_element_type=F32)


def call(body, out_shape, scratch=(), vmem=VMEM, **more):
    return pl.pallas_call(
        body,
        out_shape=out_shape,
        scratch_shapes=scratch,
        compiler_params=pltpu.CompilerParams(vmem_limit_bytes=vmem),
        **more,
    )


def nt(a, b):
    return lax.dot_general(a, b, (((1,), (1,)), ((), ())), preferred_element_type=F32)


def route_body(bag_count, *refs):
    lists, (high_ref, low_ref, bagpos_ref, pos_ref, bag_ref), (held, sems) = (
        refs[:6],
        refs[6:11],
        refs[11:],
    )
    copies = [pltpu.make_async_copy(ref, held.at[i], sems.at[i]) for i, ref in enumerate(lists)]
    for copy in copies:
        copy.start()
    for copy in copies:
        copy.wait()
    owner_ref, old_owner_ref, row_ref, old_row_ref, mask_ref, index_ref = [held.at[i] for i in range(6)]
    peers = high_ref.shape[0]
    length = pos_ref.shape[2]
    samples = bag_count // FEATS
    bags = index_ref[...]
    bag_ref[...] = jnp.where(mask_ref[...] > 0, (bags & (FEATS - 1)) * samples + (bags >> 2) + 1, 0)
    chunk = 256 if length % 256 == 0 else length
    upper = ones_where(iota((chunk, chunk), 0) <= iota((chunk, chunk), 1))
    zero = jnp.zeros((LANES, length), F32)
    high_total = jnp.zeros((peers, LANES), F32)
    low_total = jnp.zeros((peers, LANES), F32)
    bag_total = jnp.zeros((peers, LANES), F32)
    for turn in range(4):
        mb = turn % 2
        own = (owner_ref if turn < 2 else old_owner_ref)[mb]
        row = (row_ref if turn < 2 else old_row_ref)[mb] + 1
        hit = own == iota((peers, length), 0)
        onehot = ones_where(hit)
        carry = jnp.zeros((peers, 1), F32)
        parts = []
        for at in range(0, length, chunk):
            counted = mm(onehot[:, at : at + chunk], upper) + carry
            carry = counted[:, chunk - 1 :]
            parts.append(counted)
        counted = jnp.concatenate(parts, axis=1)
        rank = jnp.sum(jnp.where(hit, counted, 0.0), axis=0, keepdims=True).astype(I32) - 1
        place = iota((LANES, length), 0) == rank + turn * CAP

        def spread(value):
            high = jnp.where(place, (value >> 5).astype(F32), zero).astype(BF)
            low = jnp.where(place, (value & 31).astype(F32), zero).astype(BF)
            return nt(onehot, high), nt(onehot, low)

        high, low = spread(row)
        high_total += high
        low_total += low
        if turn < 2:
            high, low = spread(bag_ref[mb])
            bag_total += high * 32.0 + low
        else:
            pos_ref[mb] = own * CAP + rank
    high_ref[...] = high_total
    low_ref[...] = low_total
    bagpos_ref[...] = bag_total.astype(I32) - 1


def gather_body(z_ref, asked_ref, *refs):
    pairs = (len(refs) - 8) // 3
    ring = 2 * pairs + 2
    halves, passed = refs[:2], refs[2 : 2 + 2 * pairs]
    swapped, far_ref = refs[2 + 2 * pairs : 2 + 3 * pairs], refs[2 + 3 * pairs]
    out_ref, wanted_ref, cols_ref, hot_ref, req_ref = refs[-5:]
    groups = out_ref.shape[0]
    half = halves[0].shape[0]
    both = 2 * CAP
    for w in range(groups):
        rows = asked_ref[w].astype(F32)
        row = (rows[:ring] * 32.0 + rows[8 : 8 + ring]).astype(I32) - 1
        req_ref[w * ring : (w + 1) * ring, :] = jnp.where(row >= 0, row ^ z_ref[1], -1)
    wanted_ref[...] = req_ref[...]
    for z in range(ring):
        part = req_ref[pl.ds(z, groups, stride=ring), :]
        part = jnp.concatenate([part, jnp.zeros((LANES - groups, LANES), I32)], axis=0)
        cols_ref[z] = part.T
    me = z_ref[0]
    for offset in range(ring):
        z = lax.rem(me - offset + ring, ring)
        cols = cols_ref[z]
        for w in range(groups):
            hot_ref[w * both : (w + 1) * both, :] = ones_where(
                cols[:both, w : w + 1] == iota((both, 2 * half), 1)
            )
        if offset == 0:
            mine, other = halves[0][...], halves[1][...]
        elif offset == ring // 2:
            mine, other = far_ref[0], far_ref[1]
        else:
            at, way = (offset - 1, 0) if offset < ring // 2 else (ring - offset - 1, 1)
            mine, other = passed[2 * at + way][...], swapped[at][way]
        found = mm(hot_ref[:, :half], mine) + mm(hot_ref[:, half:], other)
        out_ref[:, z] = found.reshape(groups, both, LANES).astype(BF)


def pool_body(bagpos_ref, reply_ref, out_ref):
    groups, ring, both, width = reply_ref.shape
    samples = out_ref.shape[0] // 2
    bags = samples * FEATS
    slots = groups * ring * CAP
    size = slots // 8
    wide = reply_ref[...].astype(F32)
    for mb in range(2):
        flat = wide[:, :, mb * CAP : (mb + 1) * CAP, :].reshape(slots, width).astype(BF)
        total = jnp.zeros((bags, width), F32)
        for at in range(0, slots, size):
            hot = ones_where(bagpos_ref[mb, :, at : at + size] == iota((bags, size), 0))
            total += mm(hot, flat[at : at + size])
        for feat in range(FEATS):
            out_ref[mb * samples : (mb + 1) * samples, feat * width : (feat + 1) * width] = total[
                feat * samples : (feat + 1) * samples
            ].astype(BF)


def tie_body(*refs):
    del refs


def tie(value, *after):
    anywhere = pl.BlockSpec(memory_space=pl.ANY)
    return call(
        tie_body,
        vmem=1024 * 1024,
        out_shape=jax.ShapeDtypeStruct(value.shape, value.dtype),
        in_specs=[anywhere] * (1 + len(after)),
        out_specs=anywhere,
        input_output_aliases={0: 0},
    )(value, *after)


def outgoing_body(pos_ref, grad_ref, high_ref, low_ref, *refs):
    out_ref = refs[-1]
    here, rows, width = out_ref.shape
    ring = high_ref.shape[0] // here
    per = ring * CAP
    length = pos_ref.shape[2]
    first = pl.program_id(0) * here * per
    pad = [jnp.zeros((8 - ring, width), F32)] if ring < 8 else []
    for w in range(here):
        placed = []
        for mb in range(2):
            hot = ones_where(pos_ref[mb] - first == iota((per, length), 0) + w * per)
            placed.append(mm(hot, grad_ref[mb]).reshape(ring, CAP, width))
        out_ref[w, : rows - 16] = jnp.concatenate(placed, axis=1).reshape(rows - 16, width).astype(BF)
        mine = slice(w * ring, (w + 1) * ring)
        out_ref[w, rows - 16 :] = jnp.concatenate(
            [high_ref[mine]] + pad + [low_ref[mine]] + pad, axis=0
        ).astype(BF)


def scatter_body(at_ref, rows_ref, grad_ref, *refs):
    ring = rows_ref.shape[0]
    groups, _, width = grad_ref.shape
    both = 2 * CAP
    out_ref = refs[-1]
    half = out_ref.shape[1]
    count = groups * both
    for offset in range(ring):
        z = lax.rem(at_ref[0] + offset, ring)
        part = grad_ref[:, pl.ds(pl.multiple_of(z * both, both), both), :].reshape(count, width)
        sums = mm(ones_where(rows_ref[z] == iota((half, count), 0) + at_ref[1]), part)
        if len(refs) > 2:
            sums += refs[0][offset]
        out_ref[offset] = sums.astype(out_ref.dtype)


def outer_body(part_ref, delta_ref, *refs):
    out_ref = refs[-1]
    units = out_ref.shape[2]
    product = lax.dot_general(
        part_ref[...], delta_ref[...], (((0,), (0,)), ((), ())), preferred_element_type=F32
    )
    for w in range(out_ref.shape[0]):
        block = product[:, w * units : (w + 1) * units]
        if len(refs) > 1:
            block += refs[0][w].astype(F32)
        out_ref[w] = block.astype(BF)


def pick_body(bag_ref, back_ref, out_ref):
    samples = back_ref.shape[0] // 2
    bags = samples * FEATS
    length = bag_ref.shape[2]
    width = back_ref.shape[1] // FEATS
    for mb in range(2):
        rows = back_ref[mb * samples : (mb + 1) * samples, :]
        grads = jnp.concatenate(
            [rows[:, feat * width : (feat + 1) * width] for feat in range(FEATS)], axis=0
        ).astype(BF)
        for at in range(0, length, LANES):
            ids = jnp.broadcast_to(bag_ref[mb, :, at : at + LANES] - 1, (LANES, LANES)).T
            hot = jnp.concatenate(
                [ones_where(ids == iota((LANES, LANES), 1) + block) for block in range(0, bags, LANES)],
                axis=1,
            )
            out_ref[mb, 0, at : at + LANES, :] = mm(hot, grads).astype(BF)


def shape_of(shape, dtype):
    return jax.ShapeDtypeStruct(shape, dtype)


def ring_of(size, shift):
    return [(i, (i + shift) % size) for i in range(size)]


def per_device(
    dense_input,
    id_owner,
    id_row,
    id_mask,
    bag_index,
    labels,
    stale_owner,
    stale_row,
    stale_grad,
    emb_table,
    grad_squares,
    bottom_first,
    bottom_bias,
    bottom_second,
    top_weight,
    top_bias,
    out_weight,
    top_squares,
):
    groups = lax.axis_size("w")
    ring = lax.axis_size("z")
    peers = groups * ring
    core = lax.axis_index("nn")
    my_z = lax.axis_index("z")
    swap = [(0, 1), (1, 0)]
    length = id_row.shape[2]
    width = emb_table.shape[1]
    table_rows = emb_table.shape[0]
    half_rows = table_rows // 2
    samples = dense_input.shape[1]

    my_half = lax.dynamic_slice_in_dim(emb_table, core * half_rows, half_rows, 0).astype(BF)
    other_half = lax.dynamic_slice_in_dim(emb_table, (1 - core) * half_rows, half_rows, 0).astype(BF)
    rounds = []
    ahead, back = my_half, my_half
    for _ in range(1, ring // 2):
        ahead = lax.ppermute(ahead, "z", ring_of(ring, 1))
        back = lax.ppermute(back, "z", ring_of(ring, -1))
        rounds.append((ahead, back))
    swapped = [lax.ppermute(jnp.stack(blocks), "nn", swap) for blocks in rounds]
    far = jnp.stack([ahead, swapped[-1][0] if swapped else other_half])
    far = lax.ppermute(far, "z", ring_of(ring, 1))

    anywhere = pl.BlockSpec(memory_space=pl.ANY)
    high, low, bagpos, old_pos, bag_or_none = call(
        functools.partial(route_body, samples * FEATS),
        (
            shape_of((peers, LANES), F32),
            shape_of((peers, LANES), F32),
            shape_of((peers, LANES), I32),
            shape_of((2, 1, length), I32),
            shape_of((2, 1, length), I32),
        ),
        (pltpu.VMEM((6, 2, 1, length), I32), pltpu.SemaphoreType.DMA((6,))),
        in_specs=[anywhere] * 6,
    )(
        id_owner.reshape(2, 1, length),
        stale_owner.reshape(2, 1, length),
        id_row,
        stale_row,
        id_mask,
        bag_index,
    )
    bag_rows = (
        bagpos[:, : 2 * CAP].reshape(peers, 2, CAP).transpose(1, 0, 2).reshape(2, 1, peers * CAP)
    )

    cut = 4
    rows = ring * 2 * CAP + 16
    square = pl.BlockSpec((peers // cut, LANES), lambda i: (i, 0))
    outgoing = call(
        outgoing_body,
        shape_of((groups, rows, width), BF),
        grid=(cut,),
        in_specs=[
            pl.BlockSpec((2, 1, length), lambda i: (0, 0, 0)),
            pl.BlockSpec((2, length, width), lambda i: (0, 0, 0)),
            square,
            square,
        ]
        + [anywhere] * 2,
        out_specs=pl.BlockSpec((groups // cut, rows, width), lambda i: (i, 0, 0)),
    )(old_pos, stale_grad.reshape(2, length, width), high, low, *(rounds[0] if rounds else (my_half, my_half)))
    if len(rounds) > 1:
        outgoing = tie(outgoing, *rounds[1])
    incoming = lax.all_to_all(outgoing, "w", split_axis=0, concat_axis=0, tiled=True)

    others = [my_half, other_half, *(block for blocks in rounds for block in blocks), *swapped, far]
    replies, wanted = call(
        gather_body,
        (
            shape_of((groups, ring, 2 * CAP, width), BF),
            shape_of((peers, LANES), I32),
        ),
        (
            pltpu.VMEM((ring, LANES, LANES), I32),
            pltpu.VMEM((groups * 2 * CAP, table_rows), BF),
            pltpu.VMEM((peers, LANES), I32),
        ),
        grid=(1,),
        in_specs=[
            pl.BlockSpec(memory_space=pltpu.SMEM),
            pl.BlockSpec((groups, 16, width), lambda i: (0, rows // 16 - 1, 0)),
        ]
        + [pl.BlockSpec(x.shape, lambda i, n=x.ndim: (0,) * n) for x in others],
        out_specs=(
            pl.BlockSpec((groups, ring, 2 * CAP, width), lambda i: (0, 0, 0, 0)),
            pl.BlockSpec((peers, LANES), lambda i: (0, 0)),
        ),
    )(jnp.stack([my_z, core * half_rows]), incoming, *others)
    here_replies = lax.all_to_all(replies, "w", split_axis=0, concat_axis=0, tiled=True)
    old_rows = (
        wanted[:, 2 * CAP : 4 * CAP]
        .reshape(groups, ring, 2 * CAP)
        .transpose(1, 0, 2)
        .reshape(ring, 1, groups * 2 * CAP)
    )

    def scatter(first, dtype, *more):
        return call(
            scatter_body,
            shape_of((ring, half_rows, width), dtype),
            in_specs=[pl.BlockSpec(memory_space=pltpu.SMEM)]
            + [pl.BlockSpec()] * (2 + len(more))
            + [anywhere],
        )(jnp.stack([my_z, jnp.full((), first, I32)]), old_rows, incoming, *more, replies)

    theirs = lax.ppermute(scatter(half_rows, F32), "nn", swap)
    ours = scatter(0, BF, theirs)
    pooled = call(
        pool_body,
        shape_of((2 * samples, FEATS * width), BF),
    )(bag_rows, here_replies)

    dense_rows = dense_input.reshape(2 * samples, dense_input.shape[2])
    label_rows = labels.reshape(2 * samples)
    hidden = jax.nn.relu(mm(dense_rows, bottom_first) + bottom_bias).astype(BF)
    bottom = jax.nn.relu(mm(hidden, bottom_second)).astype(BF)
    joined = jnp.concatenate([bottom, pooled], axis=1)
    before = mm(joined, top_weight) + top_bias
    gate = jax.nn.sigmoid(before)
    active = (before * gate).astype(BF)
    logits = mm(active, out_weight)
    logit_grad = LOSS_SCALE * (jax.nn.sigmoid(logits) - label_rows.astype(F32))
    top_delta = (
        logit_grad[:, None]
        * out_weight.astype(F32)[None, :]
        * gate
        * (1.0 + before * (1.0 - gate))
    ).astype(BF)
    split_at = bottom.shape[1]
    back_grad = nt(top_delta, top_weight[split_at:])
    row_grads = call(pick_body, shape_of((2, 1, length, width), BF))(bag_or_none, back_grad)

    inputs = joined.shape[1] // 2
    units = top_delta.shape[1] // peers

    def outer(at, *more):
        here = groups // 4
        wide = ring * units
        block = pl.BlockSpec((here, inputs, wide), lambda i: (i, 0, 0))
        return call(
            outer_body,
            shape_of((groups, inputs, wide), BF),
            grid=(4,),
            in_specs=[
                pl.BlockSpec((2 * samples, inputs), lambda i: (0, 0)),
                pl.BlockSpec((2 * samples, here * wide), lambda i: (0, i)),
            ]
            + [block] * len(more),
            out_specs=block,
        )(lax.dynamic_slice_in_dim(joined, at * inputs, inputs, 1), top_delta, *more)

    unit_part = outer(core, lax.ppermute(outer(1 - core), "nn", swap))
    ours = tie(ours, unit_part)
    unit_part = lax.all_to_all(unit_part, "w", split_axis=0, concat_axis=0, tiled=True)

    arrived = [lax.ppermute(ours[shift], "z", ring_of(ring, shift)) for shift in range(1, ring)]
    arrived[0] = tie(arrived[0], row_grads)
    half_sum = ours[0].astype(F32)
    for part in arrived:
        half_sum += part.astype(F32)
    theirs = lax.ppermute(half_sum, "nn", swap)
    row_sum = jnp.where(
        core == 0,
        jnp.concatenate([half_sum, theirs], axis=0),
        jnp.concatenate([theirs, half_sum], axis=0),
    )
    new_squares = grad_squares + row_sum * row_sum
    new_table = emb_table - LEARN_RATE * row_sum * lax.rsqrt(new_squares)

    unit_part = jnp.sum(unit_part.astype(F32), axis=0).T.astype(BF).reshape(ring, units, inputs)
    unit_part = tie(unit_part, row_grads, new_table)
    unit_part = lax.all_to_all(unit_part, "z", split_axis=0, concat_axis=0, tiled=True)
    top_grad = jnp.sum(unit_part.astype(F32), axis=0).T
    top_step = top_grad * lax.rsqrt(top_squares + top_grad * top_grad)
    return (row_grads, new_table, new_squares, top_step)


def solution(mesh, ring=RING):
    devices = mesh.devices
    fine = Mesh(devices.reshape(devices.shape[0] // ring, ring, devices.shape[1]), ("w", "z", "nn"))
    rows = ("w", "z", "nn")
    emb = ("w", "z")
    return jax.shard_map(
        per_device,
        mesh=fine,
        in_specs=(
            P(None, rows, None),
            P(None, rows, None),
            P(None, rows, None),
            P(None, rows, None),
            P(None, rows, None),
            P(None, rows),
            P(None, rows, None),
            P(None, rows, None),
            P(None, rows, None, None),
            P(emb, None),
            P(emb, None),
            P(),
            P(),
            P(),
            P(),
            P(),
            P(),
            P("nn", emb),
        ),
        out_specs=(
            P(None, rows, None, None),
            P(emb, None),
            P(emb, None),
            P("nn", emb),
        ),
        check_vma=False,
    )
```

```python
import functools

import jax
import jax.numpy as jnp
from jax import lax
from jax.experimental import pallas as pl
from jax.experimental.pallas import tpu as pltpu
from jax.sharding import Mesh, PartitionSpec as P

FEATS = 4
CAP = 24
RING = 8
LEARN_RATE = 0.1
LOSS_SCALE = 64.0
LANES = 128
PLACES = 256
VMEM = 14 * 1024 * 1024
BF = jnp.bfloat16
F32 = jnp.float32
I32 = jnp.int32


def iota(shape, axis):
    return lax.broadcasted_iota(I32, shape, axis)


def ones_where(cond):
    return jnp.where(cond, 1.0, 0.0).astype(BF)


def near(values, first, count):
    values = values - first
    return jnp.where((values >= 0) & (values < count), values, -1).astype(F32).astype(BF)


def meet(places, shape, axis):
    index = iota(shape, axis).astype(F32).astype(BF)
    return jnp.where(places == index, jnp.ones(shape, BF), jnp.zeros(shape, BF))


def hits(values, shape, axis, first=0):
    return meet(near(values, first, shape[axis]), shape, axis)


def mm(a, b):
    return jnp.dot(a, b, preferred_element_type=F32)


def call(body, out_shape, scratch=(), vmem=VMEM, **more):
    return pl.pallas_call(
        body,
        out_shape=out_shape,
        scratch_shapes=scratch,
        compiler_params=pltpu.CompilerParams(vmem_limit_bytes=vmem),
        **more,
    )


def nt(a, b):
    return lax.dot_general(a, b, (((1,), (1,)), ((), ())), preferred_element_type=F32)


def route_body(bag_count, *refs):
    lists, (high_ref, low_ref, bagpos_ref, pos_ref, bag_ref), (held, sems) = (
        refs[:6],
        refs[6:11],
        refs[11:],
    )
    copies = [pltpu.make_async_copy(ref, held.at[i], sems.at[i]) for i, ref in enumerate(lists)]
    for copy in copies:
        copy.start()
    for copy in copies:
        copy.wait()
    owner_ref, old_owner_ref, row_ref, old_row_ref, mask_ref, index_ref = [held.at[i] for i in range(6)]
    peers = high_ref.shape[0]
    length = pos_ref.shape[2]
    samples = bag_count // FEATS
    bags = index_ref[...]
    bag_ref[...] = jnp.where(mask_ref[...] > 0, (bags & (FEATS - 1)) * samples + (bags >> 2) + 1, 0)
    chunk = 256 if length % 256 == 0 else length
    upper = ones_where(iota((chunk, chunk), 0) <= iota((chunk, chunk), 1))
    zero = jnp.zeros((LANES, length), F32)
    high_total = jnp.zeros((peers, LANES), F32)
    low_total = jnp.zeros((peers, LANES), F32)
    bag_total = jnp.zeros((peers, LANES), F32)
    for turn in range(4):
        mb = turn % 2
        own = (owner_ref if turn < 2 else old_owner_ref)[mb]
        row = (row_ref if turn < 2 else old_row_ref)[mb] + 1
        hit = own == iota((peers, length), 0)
        onehot = ones_where(hit)
        carry = jnp.zeros((peers, 1), F32)
        parts = []
        for at in range(0, length, chunk):
            counted = mm(onehot[:, at : at + chunk], upper) + carry
            carry = counted[:, chunk - 1 :]
            parts.append(counted)
        counted = jnp.concatenate(parts, axis=1)
        rank = jnp.sum(jnp.where(hit, counted, 0.0), axis=0, keepdims=True).astype(I32) - 1
        place = iota((LANES, length), 0) == rank + turn * CAP

        def spread(value):
            high = jnp.where(place, (value >> 5).astype(F32), zero).astype(BF)
            low = jnp.where(place, (value & 31).astype(F32), zero).astype(BF)
            return nt(onehot, high), nt(onehot, low)

        high, low = spread(row)
        high_total += high
        low_total += low
        if turn < 2:
            high, low = spread(bag_ref[mb])
            bag_total += high * 32.0 + low
        else:
            pos_ref[mb] = own * CAP + rank
    high_ref[...] = high_total
    low_ref[...] = low_total
    bagpos_ref[...] = bag_total.astype(I32) - 1


def gather_body(z_ref, asked_ref, *refs):
    pairs = max((len(refs) - 8) // 3, 0)
    ring = 2 * pairs + 2
    halves, passed = refs[:2], refs[2 : 2 + 2 * pairs]
    *swapped, far_ref = refs[2 + 2 * pairs : -5]
    out_ref, wanted_ref, cols_ref, hot_ref, req_ref = refs[-5:]
    groups = out_ref.shape[0]
    half = halves[0].shape[0]
    both = 2 * CAP
    for w in range(groups):
        rows = asked_ref[w].astype(F32)
        row = (rows[:ring] * 32.0 + rows[8 : 8 + ring]).astype(I32) - 1
        req_ref[w * ring : (w + 1) * ring, :] = jnp.where(row >= 0, row ^ z_ref[1], -1)
    wanted_ref[...] = req_ref[...]
    for z in range(ring):
        part = req_ref[pl.ds(z, groups, stride=ring), :]
        part = jnp.concatenate([part, jnp.zeros((LANES - groups, LANES), I32)], axis=0)
        cols_ref[z] = part.T
    me = z_ref[0]
    for offset in range(ring):
        z = lax.rem(me - offset + ring, ring)
        cols = cols_ref[z]
        for at in range(0, 2 * half, PLACES):
            ids = near(cols[:both], at, PLACES)
            for w in range(groups):
                hot_ref[offset % 2, w * both : (w + 1) * both, at : at + PLACES] = meet(
                    ids[:, w : w + 1], (both, PLACES), 1
                )
        if offset == 0:
            mine, other = halves[0][...], halves[1][...]
        elif offset == ring // 2:
            mine, other = far_ref[...], swapped[0][0]
        else:
            at, way = (offset - 1, 0) if offset < ring // 2 else (ring - offset - 1, 1)
            mine, other = passed[2 * at + way][...], swapped[at][way + (at == 0)]
        hot = hot_ref[offset % 2]
        found = mm(hot[:, :half], mine) + mm(hot[:, half:], other)
        out_ref[:, z] = found.reshape(groups, both, LANES).astype(BF)


def gate_of(before):
    return 0.5 + 0.5 * jnp.tanh(0.5 * before)


def dense_body(*refs):
    bagpos_ref, reply_ref, bottom_ref, bias_ref, out_weight_ref, label_ref, weight_ref = refs[:7]
    joined_ref, delta_ref, held, slope_ref, sems = refs[-5:]
    steps, _, wide = held.shape
    copies = [
        pltpu.make_async_copy(weight_ref.at[:, pl.ds(i * wide, wide)], held.at[i], sems.at[i])
        for i in range(steps)
    ]
    for copy in copies:
        copy.start()

    groups, ring, both, width = reply_ref.shape
    samples = joined_ref.shape[0] // 2
    bags = samples * FEATS
    slots = groups * ring * CAP
    size = slots // 8
    split_at = bottom_ref.shape[1]
    reply = reply_ref[...].astype(F32)
    for mb in range(2):
        flat = reply[:, :, mb * CAP : (mb + 1) * CAP, :].reshape(slots, width).astype(BF)
        total = jnp.zeros((bags, width), F32)
        for at in range(0, slots, size):
            ids = bagpos_ref[mb, :, at : at + size]
            hot = jnp.concatenate(
                [hits(ids, (min(PLACES, bags), size), 0, low) for low in range(0, bags, PLACES)], axis=0
            )
            total += mm(hot, flat[at : at + size])
        rows = slice(mb * samples, (mb + 1) * samples)
        joined_ref[rows, :split_at] = bottom_ref[rows]
        for feat in range(FEATS):
            at = split_at + feat * width
            joined_ref[rows, at : at + width] = total[feat * samples : (feat + 1) * samples].astype(BF)

    joined = joined_ref[...]
    sums = jnp.zeros((2 * samples, LANES), F32)
    for step in range(steps):
        copies[step].wait()
        before = mm(joined, held[step]) + bias_ref[step]
        gate = gate_of(before)
        slope_ref[step] = gate * (1.0 + before * (1.0 - gate))
        terms = (before * gate).astype(BF).astype(F32) * out_weight_ref[step]
        for at in range(0, wide, LANES):
            sums += terms[:, at : at + LANES]
    logits = jnp.sum(sums, axis=1, keepdims=True)
    labels = jnp.concatenate(
        [jnp.broadcast_to(label_ref[mb : mb + 1], (LANES, samples)).T[:, :1] for mb in range(2)], axis=0
    )
    logit_grad = LOSS_SCALE * (gate_of(logits) - labels.astype(F32))
    for step in range(steps):
        delta_ref[:, step * wide : (step + 1) * wide] = (
            logit_grad * out_weight_ref[step] * slope_ref[step]
        ).astype(BF)


def tie_body(*refs):
    del refs


def tie(value, *after):
    anywhere = pl.BlockSpec(memory_space=pl.ANY)
    return call(
        tie_body,
        vmem=1024 * 1024,
        out_shape=jax.ShapeDtypeStruct(value.shape, value.dtype),
        in_specs=[anywhere] * (1 + len(after)),
        out_specs=anywhere,
        input_output_aliases={0: 0},
    )(value, *after)


def outgoing_body(pos_ref, grad_ref, high_ref, low_ref, *refs):
    out_ref = refs[-1]
    here, rows, width = out_ref.shape
    ring = high_ref.shape[0] // here
    per = ring * CAP
    length = pos_ref.shape[2]
    first = pl.program_id(0) * here * per
    pad = [jnp.zeros((8 - ring, width), F32)] if ring < 8 else []
    placed = []
    for mb in range(2):
        hot = [hits(pos_ref[mb] - first, (per, length), 0, w * per) for w in range(here)]
        placed.append(mm(jnp.concatenate(hot, axis=0), grad_ref[mb]).reshape(here * ring, CAP, width))
    placed = jnp.concatenate(placed, axis=1).reshape(here, rows - 16, width).astype(BF)
    for w in range(here):
        out_ref[w, : rows - 16] = placed[w]
        mine = slice(w * ring, (w + 1) * ring)
        out_ref[w, rows - 16 :] = jnp.concatenate(
            [high_ref[mine]] + pad + [low_ref[mine]] + pad, axis=0
        ).astype(BF)


def scatter_body(at_ref, rows_ref, grad_ref, *refs):
    ring = rows_ref.shape[0]
    groups, _, width = grad_ref.shape
    both = 2 * CAP
    out_ref = refs[-1]
    half = out_ref.shape[1]
    count = groups * both
    for offset in range(ring):
        z = lax.rem(at_ref[0] + offset, ring)
        part = grad_ref[:, pl.ds(pl.multiple_of(z * both, both), both), :].reshape(count, width)
        ids = rows_ref[z] - at_ref[1]
        hot = [hits(ids, (PLACES, count), 0, low) for low in range(0, half, PLACES)]
        sums = mm(jnp.concatenate(hot, axis=0), part)
        if len(refs) > 2:
            sums += refs[0][offset]
        out_ref[offset] = sums.astype(out_ref.dtype)


def outer_body(part_ref, delta_ref, *refs):
    out_ref = refs[-1]
    units = out_ref.shape[2]
    product = lax.dot_general(
        part_ref[...], delta_ref[...], (((0,), (0,)), ((), ())), preferred_element_type=F32
    )
    for w in range(out_ref.shape[0]):
        block = product[:, w * units : (w + 1) * units]
        if len(refs) > 1:
            block += refs[0][w].astype(F32)
        out_ref[w] = block.astype(BF)


def pick_body(bag_ref, back_ref, out_ref):
    samples = back_ref.shape[0] // 2
    bags = samples * FEATS
    length = bag_ref.shape[2]
    width = back_ref.shape[1] // FEATS
    for mb in range(2):
        rows = back_ref[mb * samples : (mb + 1) * samples, :]
        grads = jnp.concatenate(
            [rows[:, feat * width : (feat + 1) * width] for feat in range(FEATS)], axis=0
        ).astype(BF)
        for at in range(0, length, LANES):
            ids = jnp.broadcast_to(bag_ref[mb, :, at : at + LANES] - 1, (LANES, LANES)).T
            hot = jnp.concatenate(
                [ones_where(ids == iota((LANES, LANES), 1) + block) for block in range(0, bags, LANES)],
                axis=1,
            )
            out_ref[mb, 0, at : at + LANES, :] = mm(hot, grads).astype(BF)


def shape_of(shape, dtype):
    return jax.ShapeDtypeStruct(shape, dtype)


def ring_of(size, shift):
    return [(i, (i + shift) % size) for i in range(size)]


def per_device(
    dense_input,
    id_owner,
    id_row,
    id_mask,
    bag_index,
    labels,
    stale_owner,
    stale_row,
    stale_grad,
    emb_table,
    grad_squares,
    bottom_first,
    bottom_bias,
    bottom_second,
    top_weight,
    top_bias,
    out_weight,
    top_squares,
):
    groups = lax.axis_size("w")
    ring = lax.axis_size("z")
    peers = groups * ring
    core = lax.axis_index("nn")
    my_z = lax.axis_index("z")
    swap = [(0, 1), (1, 0)]
    length = id_row.shape[2]
    width = emb_table.shape[1]
    table_rows = emb_table.shape[0]
    half_rows = table_rows // 2
    samples = dense_input.shape[1]

    my_half = lax.dynamic_slice_in_dim(emb_table, core * half_rows, half_rows, 0).astype(BF)
    other_half = lax.dynamic_slice_in_dim(emb_table, (1 - core) * half_rows, half_rows, 0).astype(BF)
    rounds = []
    ahead, back = my_half, my_half
    for _ in range(1, ring // 2):
        ahead = lax.ppermute(ahead, "z", ring_of(ring, 1))
        back = lax.ppermute(back, "z", ring_of(ring, -1))
        rounds.append((ahead, back))
    far = lax.ppermute(my_half, "z", ring_of(ring, ring // 2))
    swapped = [lax.ppermute(jnp.stack(blocks), "nn", swap) for blocks in [(far, *rounds[0]), *rounds[1:]]] if rounds else [lax.ppermute(far[None], "nn", swap)]

    anywhere = pl.BlockSpec(memory_space=pl.ANY)
    main = pl.BlockSpec(memory_space=pltpu.HBM)
    high, low, bagpos, old_pos, bag_or_none = call(
        functools.partial(route_body, samples * FEATS),
        (
            shape_of((peers, LANES), F32),
            shape_of((peers, LANES), F32),
            shape_of((peers, LANES), I32),
            shape_of((2, 1, length), I32),
            shape_of((2, 1, length), I32),
        ),
        (pltpu.VMEM((6, 2, 1, length), I32), pltpu.SemaphoreType.DMA((6,))),
        in_specs=[main] * 6,
    )(
        *(
            pltpu.with_memory_space_constraint(x.reshape(2, 1, length), pltpu.HBM)
            for x in (id_owner, stale_owner, id_row, stale_row, id_mask, bag_index)
        )
    )
    bag_rows = (
        bagpos[:, : 2 * CAP].reshape(peers, 2, CAP).transpose(1, 0, 2).reshape(2, 1, peers * CAP)
    )

    cut = 4
    rows = ring * 2 * CAP + 16
    square = pl.BlockSpec((peers // cut, LANES), lambda i: (i, 0))
    outgoing = call(
        outgoing_body,
        shape_of((groups, rows, width), BF),
        grid=(cut,),
        in_specs=[
            pl.BlockSpec((2, 1, length), lambda i: (0, 0, 0)),
            pl.BlockSpec((2, length, width), lambda i: (0, 0, 0)),
            square,
            square,
        ]
        + [],
        out_specs=pl.BlockSpec((groups // cut, rows, width), lambda i: (i, 0, 0)),
    )(old_pos, stale_grad.reshape(2, length, width), high, low)
    if rounds:
        outgoing = tie(outgoing, *rounds[0], far)
    incoming = lax.all_to_all(outgoing, "w", split_axis=0, concat_axis=0, tiled=True)

    others = [my_half, other_half, *(block for blocks in rounds for block in blocks), *swapped, far]
    replies, wanted = call(
        gather_body,
        (
            shape_of((groups, ring, 2 * CAP, width), BF),
            shape_of((peers, LANES), I32),
        ),
        (
            pltpu.VMEM((ring, LANES, LANES), I32),
            pltpu.VMEM((2, groups * 2 * CAP, table_rows), BF),
            pltpu.VMEM((peers, LANES), I32),
        ),
        grid=(1,),
        in_specs=[
            pl.BlockSpec(memory_space=pltpu.SMEM),
            pl.BlockSpec((groups, 16, width), lambda i: (0, rows // 16 - 1, 0)),
        ]
        + [pl.BlockSpec(x.shape, lambda i, n=x.ndim: (0,) * n) for x in others],
        out_specs=(
            pl.BlockSpec((groups, ring, 2 * CAP, width), lambda i: (0, 0, 0, 0)),
            pl.BlockSpec((peers, LANES), lambda i: (0, 0)),
        ),
    )(jnp.stack([my_z, core * half_rows]), incoming, *others)
    here_replies = lax.all_to_all(replies, "w", split_axis=0, concat_axis=0, tiled=True)
    old_rows = (
        wanted[:, 2 * CAP : 4 * CAP]
        .reshape(groups, ring, 2 * CAP)
        .transpose(1, 0, 2)
        .reshape(ring, 1, groups * 2 * CAP)
    )


    def scatter(first, dtype, *more):
        return call(
            scatter_body,
            shape_of((ring, half_rows, width), dtype),
            in_specs=[pl.BlockSpec(memory_space=pltpu.SMEM)]
            + [pl.BlockSpec()] * (2 + len(more))
            + [anywhere],
        )(jnp.stack([my_z, jnp.full((), first, I32)]), old_rows, incoming, *more, replies)

    theirs = lax.ppermute(scatter(half_rows, F32), "nn", swap)
    ours = scatter(0, BF, theirs)
    dense_rows = dense_input.reshape(2 * samples, dense_input.shape[2])
    hidden = jax.nn.relu(mm(dense_rows, bottom_first) + bottom_bias).astype(BF)
    bottom = jax.nn.relu(mm(hidden, bottom_second)).astype(BF)
    steps = 8
    hidden_units = top_weight.shape[1]
    wide = hidden_units // steps
    joined, top_delta = call(
        dense_body,
        (
            shape_of((2 * samples, top_weight.shape[0]), BF),
            shape_of((2 * samples, hidden_units), BF),
        ),
        (
            pltpu.VMEM((steps, top_weight.shape[0], wide), BF),
            pltpu.VMEM((steps, 2 * samples, wide), F32),
            pltpu.SemaphoreType.DMA((steps,)),
        ),
        vmem=32 * 1024 * 1024,
        in_specs=[pl.BlockSpec()] * 6 + [main],
    )(
        bag_rows,
        here_replies,
        bottom,
        top_bias.reshape(steps, 1, wide),
        out_weight.astype(F32).reshape(steps, 1, wide),
        labels,
        pltpu.with_memory_space_constraint(top_weight, pltpu.HBM),
    )
    split_at = bottom.shape[1]
    back_grad = nt(top_delta, top_weight[split_at:])
    row_grads = call(pick_body, shape_of((2, 1, length, width), BF))(bag_or_none, back_grad)

    inputs = joined.shape[1] // 2
    units = top_delta.shape[1] // peers

    def outer(at, *more):
        here = groups // 4
        wide = ring * units
        block = pl.BlockSpec((here, inputs, wide), lambda i: (i, 0, 0))
        return call(
            outer_body,
            shape_of((groups, inputs, wide), BF),
            grid=(4,),
            in_specs=[
                pl.BlockSpec((2 * samples, inputs), lambda i: (0, 0)),
                pl.BlockSpec((2 * samples, here * wide), lambda i: (0, i)),
            ]
            + [block] * len(more),
            out_specs=block,
        )(lax.dynamic_slice_in_dim(joined, at * inputs, inputs, 1), top_delta, *more)

    unit_part = outer(core, lax.ppermute(outer(1 - core), "nn", swap))
    ours = tie(ours, unit_part)
    unit_part = lax.all_to_all(unit_part, "w", split_axis=0, concat_axis=0, tiled=True)

    arrived = [lax.ppermute(ours[shift], "z", ring_of(ring, shift)) for shift in range(1, ring)]
    arrived[0] = tie(arrived[0], row_grads)
    half_sum = ours[0].astype(F32)
    for part in arrived:
        half_sum += part.astype(F32)
    theirs = lax.ppermute(half_sum, "nn", swap)
    row_sum = jnp.where(
        core == 0,
        jnp.concatenate([half_sum, theirs], axis=0),
        jnp.concatenate([theirs, half_sum], axis=0),
    )
    new_squares = grad_squares + row_sum * row_sum
    new_table = emb_table - LEARN_RATE * row_sum * lax.rsqrt(new_squares)

    unit_part = jnp.sum(unit_part.astype(F32), axis=0).T.astype(BF).reshape(ring, units, inputs)
    unit_part = tie(unit_part, row_grads, new_table)
    unit_part = lax.all_to_all(unit_part, "z", split_axis=0, concat_axis=0, tiled=True)
    top_grad = jnp.sum(unit_part.astype(F32), axis=0).T
    top_step = top_grad * lax.rsqrt(top_squares + top_grad * top_grad)
    return (row_grads, new_table, new_squares, top_step)


def solution(mesh, ring=RING):
    devices = mesh.devices
    fine = Mesh(devices.reshape(devices.shape[0] // ring, ring, devices.shape[1]), ("w", "z", "nn"))
    rows = ("w", "z", "nn")
    emb = ("w", "z")
    return jax.shard_map(
        per_device,
        mesh=fine,
        in_specs=(
            P(None, rows, None),
            P(None, rows, None),
            P(None, rows, None),
            P(None, rows, None),
            P(None, rows, None),
            P(None, rows),
            P(None, rows, None),
            P(None, rows, None),
            P(None, rows, None, None),
            P(emb, None),
            P(emb, None),
            P(),
            P(),
            P(),
            P(),
            P(),
            P(),
            P("nn", emb),
        ),
        out_specs=(
            P(None, rows, None, None),
            P(emb, None),
            P(emb, None),
            P("nn", emb),
        ),
        check_vma=False,
    )
```

```python
import functools

import jax
import jax.numpy as jnp
from jax import lax
from jax.experimental import pallas as pl
from jax.experimental.pallas import tpu as pltpu
from jax.sharding import Mesh, PartitionSpec as P

FEATS = 4
CAP = 24
RING = 8
LEARN_RATE = 0.1
LOSS_SCALE = 64.0
LANES = 128
PLACES = 256
VMEM = 14 * 1024 * 1024
BF = jnp.bfloat16
F32 = jnp.float32
I32 = jnp.int32


def iota(shape, axis):
    return lax.broadcasted_iota(I32, shape, axis)


def ones_where(cond):
    return jnp.where(cond, 1.0, 0.0).astype(BF)


def near(values, first, count):
    values = values - first
    return jnp.where((values >= 0) & (values < count), values, -1).astype(F32).astype(BF)


def meet(places, shape, axis):
    index = iota(shape, axis).astype(F32).astype(BF)
    return jnp.where(places == index, jnp.ones(shape, BF), jnp.zeros(shape, BF))


def hits(values, shape, axis, first=0):
    return meet(near(values, first, shape[axis]), shape, axis)


def mm(a, b):
    return jnp.dot(a, b, preferred_element_type=F32)


def call(body, out_shape, scratch=(), vmem=VMEM, **more):
    return pl.pallas_call(
        body,
        out_shape=out_shape,
        scratch_shapes=scratch,
        compiler_params=pltpu.CompilerParams(vmem_limit_bytes=vmem),
        **more,
    )


def nt(a, b):
    return lax.dot_general(a, b, (((1,), (1,)), ((), ())), preferred_element_type=F32)


def route_body(bag_count, *refs):
    lists, (high_ref, low_ref, bagpos_ref, pos_ref, bag_ref), (held, sems) = (
        refs[:6],
        refs[6:11],
        refs[11:],
    )
    copies = [pltpu.make_async_copy(ref, held.at[i], sems.at[i]) for i, ref in enumerate(lists)]
    for copy in copies:
        copy.start()
    for copy in copies:
        copy.wait()
    owner_ref, old_owner_ref, row_ref, old_row_ref, mask_ref, index_ref = [held.at[i] for i in range(6)]
    peers = high_ref.shape[0]
    length = pos_ref.shape[2]
    samples = bag_count // FEATS
    bags = index_ref[...]
    bag_ref[...] = jnp.where(mask_ref[...] > 0, (bags & (FEATS - 1)) * samples + (bags >> 2) + 1, 0)
    chunk = 256 if length % 256 == 0 else length
    upper = ones_where(iota((chunk, chunk), 0) <= iota((chunk, chunk), 1))
    zero = jnp.zeros((LANES, length), F32)
    high_total = jnp.zeros((peers, LANES), F32)
    low_total = jnp.zeros((peers, LANES), F32)
    bag_total = jnp.zeros((peers, LANES), F32)
    for turn in range(4):
        mb = turn % 2
        own = (owner_ref if turn < 2 else old_owner_ref)[mb]
        row = (row_ref if turn < 2 else old_row_ref)[mb] + 1
        hit = own == iota((peers, length), 0)
        onehot = ones_where(hit)
        carry = jnp.zeros((peers, 1), F32)
        parts = []
        for at in range(0, length, chunk):
            counted = mm(onehot[:, at : at + chunk], upper) + carry
            carry = counted[:, chunk - 1 :]
            parts.append(counted)
        counted = jnp.concatenate(parts, axis=1)
        rank = jnp.sum(jnp.where(hit, counted, 0.0), axis=0, keepdims=True).astype(I32) - 1
        place = iota((LANES, length), 0) == rank + turn * CAP

        def spread(value):
            high = jnp.where(place, (value >> 5).astype(F32), zero).astype(BF)
            low = jnp.where(place, (value & 31).astype(F32), zero).astype(BF)
            return nt(onehot, high), nt(onehot, low)

        high, low = spread(row)
        high_total += high
        low_total += low
        if turn < 2:
            high, low = spread(bag_ref[mb])
            bag_total += high * 32.0 + low
        else:
            pos_ref[mb] = own * CAP + rank
    high_ref[...] = high_total
    low_ref[...] = low_total
    bagpos_ref[...] = bag_total.astype(I32) - 1


def gather_body(z_ref, asked_ref, *refs):
    pairs = max((len(refs) - 8) // 3, 0)
    ring = 2 * pairs + 2
    halves, passed = refs[:2], refs[2 : 2 + 2 * pairs]
    *swapped, far_ref = refs[2 + 2 * pairs : -5]
    out_ref, wanted_ref, cols_ref, hot_ref, req_ref = refs[-5:]
    groups = out_ref.shape[0]
    half = halves[0].shape[0]
    both = 2 * CAP
    for w in range(groups):
        rows = asked_ref[w].astype(F32)
        row = (rows[:ring] * 32.0 + rows[8 : 8 + ring]).astype(I32) - 1
        req_ref[w * ring : (w + 1) * ring, :] = jnp.where(row >= 0, row ^ z_ref[1], -1)
    wanted_ref[...] = req_ref[...]
    for z in range(ring):
        part = req_ref[pl.ds(z, groups, stride=ring), :]
        part = jnp.concatenate([part, jnp.zeros((LANES - groups, LANES), I32)], axis=0)
        cols_ref[z] = part.T
    me = z_ref[0]
    for offset in range(ring):
        z = lax.rem(me - offset + ring, ring)
        cols = cols_ref[z]
        for at in range(0, 2 * half, PLACES):
            ids = near(cols[:both], at, PLACES)
            for w in range(groups):
                hot_ref[offset % 2, w * both : (w + 1) * both, at : at + PLACES] = meet(
                    ids[:, w : w + 1], (both, PLACES), 1
                )
        if offset == 0:
            mine, other = halves[0][...], halves[1][...]
        elif offset == ring // 2:
            mine, other = far_ref[...], swapped[0][0]
        else:
            at, way = (offset - 1, 0) if offset < ring // 2 else (ring - offset - 1, 1)
            mine, other = passed[2 * at + way][...], swapped[at][way + (at == 0)]
        hot = hot_ref[offset % 2]
        found = mm(hot[:, :half], mine) + mm(hot[:, half:], other)
        out_ref[:, z] = found.reshape(groups, both, LANES).astype(BF)


def gate_of(before):
    return 0.5 + 0.5 * jnp.tanh(0.5 * before)


def dense_body(*refs):
    bagpos_ref, reply_ref, bottom_ref, bias_ref, out_weight_ref, label_ref, weight_ref = refs[:7]
    joined_ref, delta_ref, held, slope_ref, sems = refs[-5:]
    steps, _, wide = held.shape
    copies = [
        pltpu.make_async_copy(weight_ref.at[:, pl.ds(i * wide, wide)], held.at[i], sems.at[i])
        for i in range(steps)
    ]
    for copy in copies:
        copy.start()

    groups, ring, both, width = reply_ref.shape
    samples = joined_ref.shape[0] // 2
    bags = samples * FEATS
    slots = groups * ring * CAP
    size = slots // 8
    split_at = bottom_ref.shape[1]
    reply = reply_ref[...].astype(F32)
    for mb in range(2):
        flat = reply[:, :, mb * CAP : (mb + 1) * CAP, :].reshape(slots, width).astype(BF)
        total = jnp.zeros((bags, width), F32)
        for at in range(0, slots, size):
            ids = bagpos_ref[mb, :, at : at + size]
            hot = jnp.concatenate(
                [hits(ids, (min(PLACES, bags), size), 0, low) for low in range(0, bags, PLACES)], axis=0
            )
            total += mm(hot, flat[at : at + size])
        rows = slice(mb * samples, (mb + 1) * samples)
        joined_ref[rows, :split_at] = bottom_ref[rows]
        for feat in range(FEATS):
            at = split_at + feat * width
            joined_ref[rows, at : at + width] = total[feat * samples : (feat + 1) * samples].astype(BF)

    joined = joined_ref[...]
    sums = jnp.zeros((2 * samples, LANES), F32)
    for step in range(steps):
        copies[step].wait()
        before = mm(joined, held[step]) + bias_ref[step]
        gate = gate_of(before)
        slope_ref[step] = gate * (1.0 + before * (1.0 - gate))
        terms = (before * gate).astype(BF).astype(F32) * out_weight_ref[step]
        for at in range(0, wide, LANES):
            sums += terms[:, at : at + LANES]
    logits = jnp.sum(sums, axis=1, keepdims=True)
    labels = jnp.concatenate(
        [jnp.broadcast_to(label_ref[mb : mb + 1], (LANES, samples)).T[:, :1] for mb in range(2)], axis=0
    )
    logit_grad = LOSS_SCALE * (gate_of(logits) - labels.astype(F32))
    for step in range(steps):
        delta_ref[:, step * wide : (step + 1) * wide] = (
            logit_grad * out_weight_ref[step] * slope_ref[step]
        ).astype(BF)


def tie_body(*refs):
    del refs


def tie(value, *after):
    anywhere = pl.BlockSpec(memory_space=pl.ANY)
    return call(
        tie_body,
        vmem=1024 * 1024,
        out_shape=jax.ShapeDtypeStruct(value.shape, value.dtype),
        in_specs=[anywhere] * (1 + len(after)),
        out_specs=anywhere,
        input_output_aliases={0: 0},
    )(value, *after)


def outgoing_body(pos_ref, grad_ref, high_ref, low_ref, *refs):
    out_ref = refs[-1]
    here, rows, width = out_ref.shape
    ring = high_ref.shape[0] // here
    per = ring * CAP
    length = pos_ref.shape[2]
    first = pl.program_id(0) * here * per
    pad = [jnp.zeros((8 - ring, width), F32)] if ring < 8 else []
    placed = []
    for mb in range(2):
        hot = [hits(pos_ref[mb] - first, (per, length), 0, w * per) for w in range(here)]
        placed.append(mm(jnp.concatenate(hot, axis=0), grad_ref[mb]).reshape(here * ring, CAP, width))
    placed = jnp.concatenate(placed, axis=1).reshape(here, rows - 16, width).astype(BF)
    for w in range(here):
        out_ref[w, : rows - 16] = placed[w]
        mine = slice(w * ring, (w + 1) * ring)
        out_ref[w, rows - 16 :] = jnp.concatenate(
            [high_ref[mine]] + pad + [low_ref[mine]] + pad, axis=0
        ).astype(BF)


def scatter_body(at_ref, rows_ref, grad_ref, *refs):
    ring = rows_ref.shape[0]
    groups, _, width = grad_ref.shape
    both = 2 * CAP
    out_ref = refs[-1]
    half = out_ref.shape[1]
    count = groups * both
    for offset in range(ring):
        z = lax.rem(at_ref[0] + offset, ring)
        part = grad_ref[:, pl.ds(pl.multiple_of(z * both, both), both), :].reshape(count, width)
        ids = rows_ref[z] - at_ref[1]
        hot = [hits(ids, (PLACES, count), 0, low) for low in range(0, half, PLACES)]
        sums = mm(jnp.concatenate(hot, axis=0), part)
        if len(refs) > 2:
            sums += refs[0][offset]
        out_ref[offset] = sums.astype(out_ref.dtype)


def outer_body(part_ref, delta_ref, *refs):
    out_ref = refs[-1]
    units = out_ref.shape[2]
    product = lax.dot_general(
        part_ref[...], delta_ref[...], (((0,), (0,)), ((), ())), preferred_element_type=F32
    )
    for w in range(out_ref.shape[0]):
        block = product[:, w * units : (w + 1) * units]
        if len(refs) > 1:
            block += refs[0][w].astype(F32)
        out_ref[w] = block.astype(BF)


def pick_body(bag_ref, back_ref, out_ref):
    samples = back_ref.shape[0] // 2
    bags = samples * FEATS
    length = bag_ref.shape[2]
    width = back_ref.shape[1] // FEATS
    for mb in range(2):
        rows = back_ref[mb * samples : (mb + 1) * samples, :]
        grads = jnp.concatenate(
            [rows[:, feat * width : (feat + 1) * width] for feat in range(FEATS)], axis=0
        ).astype(BF)
        for at in range(0, length, LANES):
            ids = jnp.broadcast_to(bag_ref[mb, :, at : at + LANES] - 1, (LANES, LANES)).T
            hot = jnp.concatenate(
                [ones_where(ids == iota((LANES, LANES), 1) + block) for block in range(0, bags, LANES)],
                axis=1,
            )
            out_ref[mb, 0, at : at + LANES, :] = mm(hot, grads).astype(BF)


def shape_of(shape, dtype):
    return jax.ShapeDtypeStruct(shape, dtype)


def ring_of(size, shift):
    return [(i, (i + shift) % size) for i in range(size)]


def per_device(
    dense_input,
    id_owner,
    id_row,
    id_mask,
    bag_index,
    labels,
    stale_owner,
    stale_row,
    stale_grad,
    emb_table,
    grad_squares,
    bottom_first,
    bottom_bias,
    bottom_second,
    top_weight,
    top_bias,
    out_weight,
    top_squares,
):
    groups = lax.axis_size("w")
    ring = lax.axis_size("z")
    peers = groups * ring
    core = lax.axis_index("nn")
    my_z = lax.axis_index("z")
    swap = [(0, 1), (1, 0)]
    length = id_row.shape[2]
    width = emb_table.shape[1]
    table_rows = emb_table.shape[0]
    half_rows = table_rows // 2
    samples = dense_input.shape[1]

    my_half = lax.dynamic_slice_in_dim(emb_table, core * half_rows, half_rows, 0).astype(BF)
    other_half = lax.dynamic_slice_in_dim(emb_table, (1 - core) * half_rows, half_rows, 0).astype(BF)
    rounds = []
    ahead, back = my_half, my_half
    for _ in range(1, ring // 2):
        ahead = lax.ppermute(ahead, "z", ring_of(ring, 1))
        back = lax.ppermute(back, "z", ring_of(ring, -1))
        rounds.append((ahead, back))
    far = lax.ppermute(my_half, "z", ring_of(ring, ring // 2))
    swapped = [lax.ppermute(jnp.stack(blocks), "nn", swap) for blocks in [(far, *rounds[0]), *rounds[1:]]] if rounds else [lax.ppermute(far[None], "nn", swap)]

    anywhere = pl.BlockSpec(memory_space=pl.ANY)
    main = pl.BlockSpec(memory_space=pltpu.HBM)
    high, low, bagpos, old_pos, bag_or_none = call(
        functools.partial(route_body, samples * FEATS),
        (
            shape_of((peers, LANES), F32),
            shape_of((peers, LANES), F32),
            shape_of((peers, LANES), I32),
            shape_of((2, 1, length), I32),
            shape_of((2, 1, length), I32),
        ),
        (pltpu.VMEM((6, 2, 1, length), I32), pltpu.SemaphoreType.DMA((6,))),
        in_specs=[main] * 6,
    )(
        *(
            pltpu.with_memory_space_constraint(x.reshape(2, 1, length), pltpu.HBM)
            for x in (id_owner, stale_owner, id_row, stale_row, id_mask, bag_index)
        )
    )
    bag_rows = (
        bagpos[:, : 2 * CAP].reshape(peers, 2, CAP).transpose(1, 0, 2).reshape(2, 1, peers * CAP)
    )

    cut = 4
    rows = ring * 2 * CAP + 16
    square = pl.BlockSpec((peers // cut, LANES), lambda i: (i, 0))
    outgoing = call(
        outgoing_body,
        shape_of((groups, rows, width), BF),
        grid=(cut,),
        in_specs=[
            pl.BlockSpec((2, 1, length), lambda i: (0, 0, 0)),
            pl.BlockSpec((2, length, width), lambda i: (0, 0, 0)),
            square,
            square,
        ]
        + [],
        out_specs=pl.BlockSpec((groups // cut, rows, width), lambda i: (i, 0, 0)),
    )(old_pos, stale_grad.reshape(2, length, width), high, low)
    if rounds:
        outgoing = tie(outgoing, *rounds[0], far)
    incoming = lax.all_to_all(outgoing, "w", split_axis=0, concat_axis=0, tiled=True)

    others = [my_half, other_half, *(block for blocks in rounds for block in blocks), *swapped, far]
    replies, wanted = call(
        gather_body,
        (
            shape_of((groups, ring, 2 * CAP, width), BF),
            shape_of((peers, LANES), I32),
        ),
        (
            pltpu.VMEM((ring, LANES, LANES), I32),
            pltpu.VMEM((2, groups * 2 * CAP, table_rows), BF),
            pltpu.VMEM((peers, LANES), I32),
        ),
        grid=(1,),
        in_specs=[
            pl.BlockSpec(memory_space=pltpu.SMEM),
            pl.BlockSpec((groups, 16, width), lambda i: (0, rows // 16 - 1, 0)),
        ]
        + [pl.BlockSpec(x.shape, lambda i, n=x.ndim: (0,) * n) for x in others],
        out_specs=(
            pl.BlockSpec((groups, ring, 2 * CAP, width), lambda i: (0, 0, 0, 0)),
            pl.BlockSpec((peers, LANES), lambda i: (0, 0)),
        ),
    )(jnp.stack([my_z, core * half_rows]), incoming, *others)
    here_replies = lax.all_to_all(replies, "w", split_axis=0, concat_axis=0, tiled=True)
    old_rows = (
        wanted[:, 2 * CAP : 4 * CAP]
        .reshape(groups, ring, 2 * CAP)
        .transpose(1, 0, 2)
        .reshape(ring, 1, groups * 2 * CAP)
    )


    def scatter(first, dtype, *more):
        return call(
            scatter_body,
            shape_of((ring, half_rows, width), dtype),
            vmem=10 * 1024 * 1024,
            in_specs=[pl.BlockSpec(memory_space=pltpu.SMEM)]
            + [pl.BlockSpec()] * (2 + len(more))
            + [anywhere],
        )(jnp.stack([my_z, jnp.full((), first, I32)]), old_rows, incoming, *more, replies)

    leaving = scatter(half_rows, F32)
    theirs = lax.ppermute(leaving, "nn", swap)
    ours = scatter(0, BF, theirs)
    dense_rows = dense_input.reshape(2 * samples, dense_input.shape[2])
    hidden = jax.nn.relu(mm(dense_rows, bottom_first) + bottom_bias).astype(BF)
    bottom = jax.nn.relu(mm(hidden, bottom_second)).astype(BF)
    steps = 8
    hidden_units = top_weight.shape[1]
    wide = hidden_units // steps
    joined, top_delta = call(
        dense_body,
        (
            shape_of((2 * samples, top_weight.shape[0]), BF),
            shape_of((2 * samples, hidden_units), BF),
        ),
        (
            pltpu.VMEM((steps, top_weight.shape[0], wide), BF),
            pltpu.VMEM((steps, 2 * samples, wide), F32),
            pltpu.SemaphoreType.DMA((steps,)),
        ),
        vmem=24 * 1024 * 1024,
        in_specs=[pl.BlockSpec()] * 6 + [main, anywhere],
    )(
        bag_rows,
        here_replies,
        bottom,
        top_bias.reshape(steps, 1, wide),
        out_weight.astype(F32).reshape(steps, 1, wide),
        labels,
        pltpu.with_memory_space_constraint(top_weight, pltpu.HBM),
        leaving,
    )
    split_at = bottom.shape[1]
    back_grad = nt(top_delta, top_weight[split_at:])
    row_grads = call(pick_body, shape_of((2, 1, length, width), BF), vmem=8 * 1024 * 1024)(bag_or_none, back_grad)

    inputs = joined.shape[1] // 2
    units = top_delta.shape[1] // peers

    def outer(at, *more):
        here = groups // 4
        wide = ring * units
        block = pl.BlockSpec((here, inputs, wide), lambda i: (i, 0, 0))
        return call(
            outer_body,
            shape_of((groups, inputs, wide), BF),
            vmem=8 * 1024 * 1024,
            grid=(4,),
            in_specs=[
                pl.BlockSpec((2 * samples, inputs), lambda i: (0, 0)),
                pl.BlockSpec((2 * samples, here * wide), lambda i: (0, i)),
            ]
            + [block, anywhere][: len(more)],
            out_specs=block,
        )(lax.dynamic_slice_in_dim(joined, at * inputs, inputs, 1), top_delta, *more)

    unit_part = outer(core, lax.ppermute(outer(1 - core), "nn", swap))
    ours = tie(ours, unit_part)
    unit_part = lax.all_to_all(unit_part, "w", split_axis=0, concat_axis=0, tiled=True)

    arrived = [lax.ppermute(ours[shift], "z", ring_of(ring, shift)) for shift in range(1, ring)]
    arrived[0] = tie(arrived[0], row_grads)
    half_sum = ours[0].astype(F32)
    for part in arrived:
        half_sum += part.astype(F32)
    theirs = lax.ppermute(half_sum, "nn", swap)
    row_sum = jnp.where(
        core == 0,
        jnp.concatenate([half_sum, theirs], axis=0),
        jnp.concatenate([theirs, half_sum], axis=0),
    )
    new_squares = grad_squares + row_sum * row_sum
    new_table = emb_table - LEARN_RATE * row_sum * lax.rsqrt(new_squares)

    unit_part = jnp.sum(unit_part.astype(F32), axis=0).T.astype(BF).reshape(ring, units, inputs)
    unit_part = tie(unit_part, row_grads)
    unit_part = lax.all_to_all(unit_part, "z", split_axis=0, concat_axis=0, tiled=True)
    top_grad = jnp.sum(unit_part.astype(F32), axis=0).T
    top_step = top_grad * lax.rsqrt(top_squares + top_grad * top_grad)
    return (row_grads, new_table, new_squares, top_step)


def solution(mesh, ring=RING):
    devices = mesh.devices
    fine = Mesh(devices.reshape(devices.shape[0] // ring, ring, devices.shape[1]), ("w", "z", "nn"))
    rows = ("w", "z", "nn")
    emb = ("w", "z")
    return jax.shard_map(
        per_device,
        mesh=fine,
        in_specs=(
            P(None, rows, None),
            P(None, rows, None),
            P(None, rows, None),
            P(None, rows, None),
            P(None, rows, None),
            P(None, rows),
            P(None, rows, None),
            P(None, rows, None),
            P(None, rows, None, None),
            P(emb, None),
            P(emb, None),
            P(),
            P(),
            P(),
            P(),
            P(),
            P(),
            P("nn", emb),
        ),
        out_specs=(
            P(None, rows, None, None),
            P(emb, None),
            P(emb, None),
            P("nn", emb),
        ),
        check_vma=False,
    )
```

```python
import functools

import jax
import jax.numpy as jnp
from jax import lax
from jax.experimental import pallas as pl
from jax.experimental.pallas import tpu as pltpu
from jax.sharding import Mesh, PartitionSpec as P

FEATS = 4
CAP = 24
RING = 8
LEARN_RATE = 0.1
LOSS_SCALE = 64.0
LANES = 128
PLACES = 256
VMEM = 14 * 1024 * 1024
BF = jnp.bfloat16
F32 = jnp.float32
I32 = jnp.int32


def iota(shape, axis):
    return lax.broadcasted_iota(I32, shape, axis)


def ones_where(cond):
    return jnp.where(cond, 1.0, 0.0).astype(BF)


def near(values, first, count):
    values = values - first
    return jnp.where((values >= 0) & (values < count), values, -1).astype(F32).astype(BF)


def meet(places, shape, axis):
    index = iota(shape, axis).astype(F32).astype(BF)
    return jnp.where(places == index, jnp.ones(shape, BF), jnp.zeros(shape, BF))


def hits(values, shape, axis, first=0):
    return meet(near(values, first, shape[axis]), shape, axis)


def mm(a, b):
    return jnp.dot(a, b, preferred_element_type=F32)


def call(body, out_shape, scratch=(), vmem=VMEM, **more):
    return pl.pallas_call(
        body,
        out_shape=out_shape,
        scratch_shapes=scratch,
        compiler_params=pltpu.CompilerParams(vmem_limit_bytes=vmem),
        **more,
    )


def nt(a, b):
    return lax.dot_general(a, b, (((1,), (1,)), ((), ())), preferred_element_type=F32)


def route_body(bag_count, *refs):
    lists, (high_ref, low_ref, bagpos_ref, pos_ref, bag_ref), (held, sems) = (
        refs[:6],
        refs[6:11],
        refs[11:],
    )
    copies = [pltpu.make_async_copy(ref, held.at[i], sems.at[i]) for i, ref in enumerate(lists)]
    for copy in copies:
        copy.start()
    for copy in copies:
        copy.wait()
    owner_ref, old_owner_ref, row_ref, old_row_ref, mask_ref, index_ref = [held.at[i] for i in range(6)]
    peers = high_ref.shape[0]
    length = pos_ref.shape[2]
    samples = bag_count // FEATS
    bags = index_ref[...]
    bag_ref[...] = jnp.where(mask_ref[...] > 0, (bags & (FEATS - 1)) * samples + (bags >> 2) + 1, 0)
    chunk = 256 if length % 256 == 0 else length
    upper = ones_where(iota((chunk, chunk), 0) <= iota((chunk, chunk), 1))
    zero = jnp.zeros((LANES, length), F32)
    high_total = jnp.zeros((peers, LANES), F32)
    low_total = jnp.zeros((peers, LANES), F32)
    bag_total = jnp.zeros((peers, LANES), F32)
    for turn in range(4):
        mb = turn % 2
        own = (owner_ref if turn < 2 else old_owner_ref)[mb]
        row = (row_ref if turn < 2 else old_row_ref)[mb] + 1
        hit = own == iota((peers, length), 0)
        onehot = ones_where(hit)
        carry = jnp.zeros((peers, 1), F32)
        parts = []
        for at in range(0, length, chunk):
            counted = mm(onehot[:, at : at + chunk], upper) + carry
            carry = counted[:, chunk - 1 :]
            parts.append(counted)
        counted = jnp.concatenate(parts, axis=1)
        rank = jnp.sum(jnp.where(hit, counted, 0.0), axis=0, keepdims=True).astype(I32) - 1
        place = iota((LANES, length), 0) == rank + turn * CAP

        def spread(value):
            high = jnp.where(place, (value >> 5).astype(F32), zero).astype(BF)
            low = jnp.where(place, (value & 31).astype(F32), zero).astype(BF)
            return nt(onehot, high), nt(onehot, low)

        high, low = spread(row)
        high_total += high
        low_total += low
        if turn < 2:
            high, low = spread(bag_ref[mb])
            bag_total += high * 32.0 + low
        else:
            pos_ref[mb] = own * CAP + rank
    high_ref[...] = high_total
    low_ref[...] = low_total
    bagpos_ref[...] = bag_total.astype(I32) - 1


def gather_body(z_ref, asked_ref, *refs):
    pairs = max((len(refs) - 8) // 3, 0)
    ring = 2 * pairs + 2
    halves, passed = refs[:2], refs[2 : 2 + 2 * pairs]
    *swapped, far_ref = refs[2 + 2 * pairs : -5]
    out_ref, wanted_ref, cols_ref, hot_ref, req_ref = refs[-5:]
    groups = out_ref.shape[0]
    half = halves[0].shape[0]
    both = 2 * CAP
    for w in range(groups):
        rows = asked_ref[w].astype(F32)
        row = (rows[:ring] * 32.0 + rows[8 : 8 + ring]).astype(I32) - 1
        req_ref[w * ring : (w + 1) * ring, :] = jnp.where(row >= 0, row ^ z_ref[1], -1)
    wanted_ref[...] = req_ref[...]
    for z in range(ring):
        part = req_ref[pl.ds(z, groups, stride=ring), :]
        part = jnp.concatenate([part, jnp.zeros((LANES - groups, LANES), I32)], axis=0)
        cols_ref[z] = part.T
    me = z_ref[0]
    for offset in range(ring):
        z = lax.rem(me - offset + ring, ring)
        cols = cols_ref[z]
        for at in range(0, 2 * half, PLACES):
            ids = near(cols[:both], at, PLACES)
            for w in range(groups):
                hot_ref[offset % 2, w * both : (w + 1) * both, at : at + PLACES] = meet(
                    ids[:, w : w + 1], (both, PLACES), 1
                )
        if offset == 0:
            mine, other = halves[0][...], halves[1][...]
        elif offset == ring // 2:
            mine, other = far_ref[...], swapped[0][0]
        else:
            at, way = (offset - 1, 0) if offset < ring // 2 else (ring - offset - 1, 1)
            mine, other = passed[2 * at + way][...], swapped[at][way + (at == 0)]
        hot = hot_ref[offset % 2]
        found = mm(hot[:, :half], mine) + mm(hot[:, half:], other)
        out_ref[:, z] = found.reshape(groups, both, LANES).astype(BF)


def gate_of(before):
    return 0.5 + 0.5 * jnp.tanh(0.5 * before)


def dense_body(*refs):
    bagpos_ref, reply_ref, bottom_ref, bias_ref, out_weight_ref, label_ref, weight_ref = refs[:7]
    joined_ref, delta_ref, held, slope_ref, sems = refs[-5:]
    steps, _, wide = held.shape
    copies = [
        pltpu.make_async_copy(weight_ref.at[:, pl.ds(i * wide, wide)], held.at[i], sems.at[i])
        for i in range(steps)
    ]
    for copy in copies:
        copy.start()

    groups, ring, both, width = reply_ref.shape
    samples = joined_ref.shape[0] // 2
    bags = samples * FEATS
    slots = groups * ring * CAP
    size = slots // 8
    split_at = bottom_ref.shape[1]
    reply = reply_ref[...].astype(F32)
    for mb in range(2):
        flat = reply[:, :, mb * CAP : (mb + 1) * CAP, :].reshape(slots, width).astype(BF)
        total = jnp.zeros((bags, width), F32)
        for at in range(0, slots, size):
            ids = bagpos_ref[mb, :, at : at + size]
            hot = jnp.concatenate(
                [hits(ids, (min(PLACES, bags), size), 0, low) for low in range(0, bags, PLACES)], axis=0
            )
            total += mm(hot, flat[at : at + size])
        rows = slice(mb * samples, (mb + 1) * samples)
        joined_ref[rows, :split_at] = bottom_ref[rows]
        for feat in range(FEATS):
            at = split_at + feat * width
            joined_ref[rows, at : at + width] = total[feat * samples : (feat + 1) * samples].astype(BF)

    joined = joined_ref[...]
    sums = jnp.zeros((2 * samples, LANES), F32)
    for step in range(steps):
        copies[step].wait()
        before = mm(joined, held[step]) + bias_ref[step]
        gate = gate_of(before)
        slope_ref[step] = gate * (1.0 + before * (1.0 - gate))
        terms = (before * gate).astype(BF).astype(F32) * out_weight_ref[step]
        for at in range(0, wide, LANES):
            sums += terms[:, at : at + LANES]
    logits = jnp.sum(sums, axis=1, keepdims=True)
    labels = jnp.concatenate(
        [jnp.broadcast_to(label_ref[mb : mb + 1], (LANES, samples)).T[:, :1] for mb in range(2)], axis=0
    )
    logit_grad = LOSS_SCALE * (gate_of(logits) - labels.astype(F32))
    for step in range(steps):
        delta_ref[:, step * wide : (step + 1) * wide] = (
            logit_grad * out_weight_ref[step] * slope_ref[step]
        ).astype(BF)


def tie_body(*refs):
    del refs


def tie(value, *after):
    anywhere = pl.BlockSpec(memory_space=pl.ANY)
    return call(
        tie_body,
        vmem=1024 * 1024,
        out_shape=jax.ShapeDtypeStruct(value.shape, value.dtype),
        in_specs=[anywhere] * (1 + len(after)),
        out_specs=anywhere,
        input_output_aliases={0: 0},
    )(value, *after)


def outgoing_body(pos_ref, grad_ref, high_ref, low_ref, *refs):
    out_ref = refs[-1]
    here, rows, width = out_ref.shape
    ring = high_ref.shape[0] // here
    per = ring * CAP
    length = pos_ref.shape[2]
    first = pl.program_id(0) * here * per
    pad = [jnp.zeros((8 - ring, width), F32)] if ring < 8 else []
    placed = []
    for mb in range(2):
        hot = [hits(pos_ref[mb] - first, (per, length), 0, w * per) for w in range(here)]
        placed.append(mm(jnp.concatenate(hot, axis=0), grad_ref[mb]).reshape(here * ring, CAP, width))
    placed = jnp.concatenate(placed, axis=1).reshape(here, rows - 16, width).astype(BF)
    for w in range(here):
        out_ref[w, : rows - 16] = placed[w]
        mine = slice(w * ring, (w + 1) * ring)
        out_ref[w, rows - 16 :] = jnp.concatenate(
            [high_ref[mine]] + pad + [low_ref[mine]] + pad, axis=0
        ).astype(BF)


def scatter_body(at_ref, rows_ref, grad_ref, *refs):
    ring = rows_ref.shape[0]
    groups, _, width = grad_ref.shape
    both = 2 * CAP
    out_ref = refs[-1]
    half = out_ref.shape[1]
    count = groups * both
    for offset in range(ring):
        z = lax.rem(at_ref[0] + offset, ring)
        part = grad_ref[:, pl.ds(pl.multiple_of(z * both, both), both), :].reshape(count, width)
        ids = rows_ref[z] - at_ref[1]
        hot = [hits(ids, (PLACES, count), 0, low) for low in range(0, half, PLACES)]
        sums = mm(jnp.concatenate(hot, axis=0), part)
        if len(refs) > 2:
            sums += refs[0][offset]
        out_ref[offset] = sums.astype(out_ref.dtype)


def outer_body(part_ref, delta_ref, *refs):
    out_ref = refs[-1]
    units = out_ref.shape[2]
    product = lax.dot_general(
        part_ref[...], delta_ref[...], (((0,), (0,)), ((), ())), preferred_element_type=F32
    )
    for w in range(out_ref.shape[0]):
        block = product[:, w * units : (w + 1) * units]
        if len(refs) > 1:
            block += refs[0][w].astype(F32)
        out_ref[w] = block.astype(BF)


def pick_body(bag_ref, back_ref, out_ref):
    samples = back_ref.shape[0] // 2
    bags = samples * FEATS
    length = bag_ref.shape[2]
    width = back_ref.shape[1] // FEATS
    for mb in range(2):
        rows = back_ref[mb * samples : (mb + 1) * samples, :]
        grads = jnp.concatenate(
            [rows[:, feat * width : (feat + 1) * width] for feat in range(FEATS)], axis=0
        ).astype(BF)
        for at in range(0, length, LANES):
            ids = jnp.broadcast_to(bag_ref[mb, :, at : at + LANES] - 1, (LANES, LANES)).T
            hot = jnp.concatenate(
                [ones_where(ids == iota((LANES, LANES), 1) + block) for block in range(0, bags, LANES)],
                axis=1,
            )
            out_ref[mb, 0, at : at + LANES, :] = mm(hot, grads).astype(BF)


def shape_of(shape, dtype):
    return jax.ShapeDtypeStruct(shape, dtype)


def ring_of(size, shift):
    return [(i, (i + shift) % size) for i in range(size)]


def per_device(
    dense_input,
    id_owner,
    id_row,
    id_mask,
    bag_index,
    labels,
    stale_owner,
    stale_row,
    stale_grad,
    emb_table,
    grad_squares,
    bottom_first,
    bottom_bias,
    bottom_second,
    top_weight,
    top_bias,
    out_weight,
    top_squares,
):
    groups = lax.axis_size("w")
    ring = lax.axis_size("z")
    peers = groups * ring
    core = lax.axis_index("nn")
    my_z = lax.axis_index("z")
    swap = [(0, 1), (1, 0)]
    length = id_row.shape[2]
    width = emb_table.shape[1]
    table_rows = emb_table.shape[0]
    half_rows = table_rows // 2
    samples = dense_input.shape[1]

    my_half = lax.dynamic_slice_in_dim(emb_table, core * half_rows, half_rows, 0).astype(BF)
    other_half = lax.dynamic_slice_in_dim(emb_table, (1 - core) * half_rows, half_rows, 0).astype(BF)
    rounds = []
    ahead, back = my_half, my_half
    for _ in range(1, ring // 2):
        ahead = lax.ppermute(ahead, "z", ring_of(ring, 1))
        back = lax.ppermute(back, "z", ring_of(ring, -1))
        rounds.append((ahead, back))
    far = lax.ppermute(my_half, "z", ring_of(ring, ring // 2))
    swapped = [lax.ppermute(jnp.stack(blocks), "nn", swap) for blocks in [(far, *rounds[0]), *rounds[1:]]] if rounds else [lax.ppermute(far[None], "nn", swap)]

    anywhere = pl.BlockSpec(memory_space=pl.ANY)
    main = pl.BlockSpec(memory_space=pltpu.HBM)
    high, low, bagpos, old_pos, bag_or_none = call(
        functools.partial(route_body, samples * FEATS),
        (
            shape_of((peers, LANES), F32),
            shape_of((peers, LANES), F32),
            shape_of((peers, LANES), I32),
            shape_of((2, 1, length), I32),
            shape_of((2, 1, length), I32),
        ),
        (pltpu.VMEM((6, 2, 1, length), I32), pltpu.SemaphoreType.DMA((6,))),
        in_specs=[main] * 6,
    )(
        *(
            pltpu.with_memory_space_constraint(x.reshape(2, 1, length), pltpu.HBM)
            for x in (id_owner, stale_owner, id_row, stale_row, id_mask, bag_index)
        )
    )
    bag_rows = (
        bagpos[:, : 2 * CAP].reshape(peers, 2, CAP).transpose(1, 0, 2).reshape(2, 1, peers * CAP)
    )

    cut = 4
    rows = ring * 2 * CAP + 16
    square = pl.BlockSpec((peers // cut, LANES), lambda i: (i, 0))
    outgoing = call(
        outgoing_body,
        shape_of((groups, rows, width), BF),
        grid=(cut,),
        in_specs=[
            pl.BlockSpec((2, 1, length), lambda i: (0, 0, 0)),
            pl.BlockSpec((2, length, width), lambda i: (0, 0, 0)),
            square,
            square,
        ]
        + [],
        out_specs=pl.BlockSpec((groups // cut, rows, width), lambda i: (i, 0, 0)),
    )(old_pos, stale_grad.reshape(2, length, width), high, low)
    if rounds:
        outgoing = tie(outgoing, *rounds[0], far)
    incoming = lax.all_to_all(outgoing, "w", split_axis=0, concat_axis=0, tiled=True)

    others = [my_half, other_half, *(block for blocks in rounds for block in blocks), *swapped, far]
    replies, wanted = call(
        gather_body,
        (
            shape_of((groups, ring, 2 * CAP, width), BF),
            shape_of((peers, LANES), I32),
        ),
        (
            pltpu.VMEM((ring, LANES, LANES), I32),
            pltpu.VMEM((2, groups * 2 * CAP, table_rows), BF),
            pltpu.VMEM((peers, LANES), I32),
        ),
        grid=(1,),
        in_specs=[
            pl.BlockSpec(memory_space=pltpu.SMEM),
            pl.BlockSpec((groups, 16, width), lambda i: (0, rows // 16 - 1, 0)),
        ]
        + [pl.BlockSpec(x.shape, lambda i, n=x.ndim: (0,) * n) for x in others],
        out_specs=(
            pl.BlockSpec((groups, ring, 2 * CAP, width), lambda i: (0, 0, 0, 0)),
            pl.BlockSpec((peers, LANES), lambda i: (0, 0)),
        ),
    )(jnp.stack([my_z, core * half_rows]), incoming, *others)
    here_replies = lax.all_to_all(replies, "w", split_axis=0, concat_axis=0, tiled=True)
    old_rows = (
        wanted[:, 2 * CAP : 4 * CAP]
        .reshape(groups, ring, 2 * CAP)
        .transpose(1, 0, 2)
        .reshape(ring, 1, groups * 2 * CAP)
    )


    def scatter(first, dtype, *more):
        return call(
            scatter_body,
            shape_of((ring, half_rows, width), dtype),
            vmem=10 * 1024 * 1024,
            in_specs=[pl.BlockSpec(memory_space=pltpu.SMEM)]
            + [pl.BlockSpec()] * (2 + len(more))
            + [anywhere],
        )(jnp.stack([my_z, jnp.full((), first, I32)]), old_rows, incoming, *more, replies)

    leaving = scatter(half_rows, F32)
    theirs = lax.ppermute(leaving, "nn", swap)
    ours = scatter(0, BF, theirs)
    dense_rows = dense_input.reshape(2 * samples, dense_input.shape[2])
    hidden = jax.nn.relu(mm(dense_rows, bottom_first) + bottom_bias).astype(BF)
    bottom = jax.nn.relu(mm(hidden, bottom_second)).astype(BF)
    steps = 8
    hidden_units = top_weight.shape[1]
    wide = hidden_units // steps
    joined, top_delta = call(
        dense_body,
        (
            shape_of((2 * samples, top_weight.shape[0]), BF),
            shape_of((2 * samples, hidden_units), BF),
        ),
        (
            pltpu.VMEM((steps, top_weight.shape[0], wide), BF),
            pltpu.VMEM((steps, 2 * samples, wide), F32),
            pltpu.SemaphoreType.DMA((steps,)),
        ),
        vmem=24 * 1024 * 1024,
        in_specs=[pl.BlockSpec()] * 6 + [main, anywhere],
    )(
        bag_rows,
        here_replies,
        bottom,
        top_bias.reshape(steps, 1, wide),
        out_weight.astype(F32).reshape(steps, 1, wide),
        labels,
        pltpu.with_memory_space_constraint(top_weight, pltpu.HBM),
        leaving,
    )
    split_at = bottom.shape[1]
    back_grad = nt(top_delta, top_weight[split_at:])
    row_grads = call(pick_body, shape_of((2, 1, length, width), BF), vmem=8 * 1024 * 1024)(bag_or_none, back_grad)

    inputs = joined.shape[1] // 2
    units = top_delta.shape[1] // peers

    def outer(at, *more):
        here = groups // 4
        wide = ring * units
        block = pl.BlockSpec((here, inputs, wide), lambda i: (i, 0, 0))
        return call(
            outer_body,
            shape_of((groups, inputs, wide), BF),
            vmem=8 * 1024 * 1024,
            grid=(4,),
            in_specs=[
                pl.BlockSpec((2 * samples, inputs), lambda i: (0, 0)),
                pl.BlockSpec((2 * samples, here * wide), lambda i: (0, i)),
            ]
            + [block, anywhere][: len(more)],
            out_specs=block,
        )(lax.dynamic_slice_in_dim(joined, at * inputs, inputs, 1), top_delta, *more)

    unit_part = outer(core, lax.ppermute(outer(1 - core), "nn", swap))
    ours = tie(ours, unit_part)
    unit_part = lax.all_to_all(unit_part, "w", split_axis=0, concat_axis=0, tiled=True)

    arrived = [lax.ppermute(ours[shift], "z", ring_of(ring, shift)) for shift in range(1, ring)]
    unit_part = jnp.sum(unit_part.astype(F32), axis=0).T.astype(BF).reshape(ring, units, inputs)
    unit_part = tie(unit_part, row_grads)
    arrived[0] = tie(arrived[0], unit_part)
    half_sum = ours[0].astype(F32)
    for part in arrived:
        half_sum += part.astype(F32)
    theirs = lax.ppermute(half_sum, "nn", swap)
    row_sum = jnp.where(
        core == 0,
        jnp.concatenate([half_sum, theirs], axis=0),
        jnp.concatenate([theirs, half_sum], axis=0),
    )
    new_squares = grad_squares + row_sum * row_sum
    new_table = emb_table - LEARN_RATE * row_sum * lax.rsqrt(new_squares)

    unit_part = lax.all_to_all(unit_part, "z", split_axis=0, concat_axis=0, tiled=True)
    top_grad = jnp.sum(unit_part.astype(F32), axis=0).T
    top_step = top_grad * lax.rsqrt(top_squares + top_grad * top_grad)
    return (row_grads, new_table, new_squares, top_step)


def solution(mesh, ring=RING):
    devices = mesh.devices
    fine = Mesh(devices.reshape(devices.shape[0] // ring, ring, devices.shape[1]), ("w", "z", "nn"))
    rows = ("w", "z", "nn")
    emb = ("w", "z")
    return jax.shard_map(
        per_device,
        mesh=fine,
        in_specs=(
            P(None, rows, None),
            P(None, rows, None),
            P(None, rows, None),
            P(None, rows, None),
            P(None, rows, None),
            P(None, rows),
            P(None, rows, None),
            P(None, rows, None),
            P(None, rows, None, None),
            P(emb, None),
            P(emb, None),
            P(),
            P(),
            P(),
            P(),
            P(),
            P(),
            P("nn", emb),
        ),
        out_specs=(
            P(None, rows, None, None),
            P(emb, None),
            P(emb, None),
            P("nn", emb),
        ),
        check_vma=False,
    )
```
